128 devices in a mesh: group: 32 (over y_lo, x, z), tensor: 4 (over y_hi, core).
Axes of the slice: x: 4, y: 4 (y_hi: 2, y_lo: 2; y = y_hi * 2 + y_lo), z: 4, core: 2. Of those that a mesh axis runs over, the one named last changes fastest.
Arguments:
- inputs: bfloat16 [2, 1024, 5120], P(None, 'group'), may hold values from -6 to 6
- attn_gain: float32 [5120], replicated, may hold values from 0.5 to 2
- w_query: bfloat16 [5120, 4096], P(None, 'tensor'), may hold values from -0.078125 to 0.078125
- key_matrix: bfloat16 [5120, 512], P(None, 'tensor'), may hold values from -0.078125 to 0.078125
- value_matrix: bfloat16 [5120, 512], P(None, 'tensor'), may hold values from -0.078125 to 0.078125
- q_gain: float32 [128], replicated, may hold values from 0.5 to 2
- k_gain: float32 [128], replicated, may hold values from 0.5 to 2
- w_out: bfloat16 [4096, 5120], P('tensor'), may hold values from -0.75 to 0.75
- prompt_key_cache: bfloat16 [64, 1024, 512], P('group', None, 'tensor'), may hold values from -820 to 820
- prompt_value_cache: bfloat16 [64, 1024, 512], P('group', None, 'tensor'), may hold values from -6 to 6
- prompt_lengths: int32 [64], replicated, may hold values from 1 to 1024, 26214 in all
- prompt_slot: int32 [64], replicated, may hold values from 0 to 63, as said below
- sample_prompt: int32 [1024], replicated, may hold values from 0 to 63, as said below
Outputs:
- attention_out: bfloat16 [2, 1024, 5120], P(None, 'group', 'tensor')
The draws below stay inside these ranges and needn't reach their ends.
Inputs may be any that keep to these rules, and one draw needn't show every extreme that they name: A permutation: prompt p's keys and values stand in row prompt_slot[p] of prompt_key_cache and prompt_value_cache. `sample_prompt`: each prompt is continued by 16 rows, 8 on each of two groups; the 32 rows of one group continue 4 prompts, 8 rows each, whose cache rows lie on 4 different groups.
All inputs are finite; a program needn't handle non-finite values.
Results may differ from the reference program's by a relative error of at most 0.03.
Values may be sent and summed in bfloat16 or wider, within the bound.
A program may use at most 128 MiB of HBM per device.

```python
import math
import jax
import jax.numpy as jnp
import numpy as np
from jax import lax

MODEL_DIM = 5120
HEAD_SIZE = 128
QUERY_HEADS = 32
KEY_HEADS = 4
READ = 4
STEPS = 2
PROMPT_SLOTS = 1024
HALF = 8
ROWS = 32
P_DEV = 2
PROMPT_COUNT = 64
SAMPLES = 1024


def placement(key):
    groups = PROMPT_COUNT // P_DEV
    slot_order = jax.random.permutation(jax.random.fold_in(key, 11), PROMPT_COUNT).astype(jnp.int32)
    prompt_of = jnp.argsort(slot_order).astype(jnp.int32)
    every_group = jnp.arange(groups, dtype=jnp.int32)
    start_group = jax.random.randint(jax.random.fold_in(key, 14), (), 0, groups).astype(jnp.int32)
    cycle_rank = jnp.argsort(jax.random.permutation(jax.random.fold_in(key, 15), groups)).astype(jnp.int32)
    cycle_score = cycle_rank + 3
    cycle_score = jnp.where(every_group == start_group, 0, cycle_score)
    cycle_score = jnp.where(every_group == (start_group + groups - 1) % groups, 1, cycle_score)
    cycle_score = jnp.where(every_group == (start_group + groups // 2) % groups, 2, cycle_score)
    cycle_list = jnp.argsort(cycle_score).astype(jnp.int32)
    cycle_place = jnp.argsort(cycle_list).astype(jnp.int32)
    offset_pool = jax.random.permutation(jax.random.fold_in(key, 12), groups).astype(jnp.int32)
    pool_score = jnp.where((offset_pool == 1) | (offset_pool == 2), groups + offset_pool, every_group)
    extra_offsets = offset_pool[jnp.argsort(pool_score)][:READ - 2]
    base_offsets = jnp.concatenate([jnp.array([1, 2], jnp.int32), extra_offsets])
    offsets = base_offsets[jax.random.permutation(jax.random.fold_in(key, 16), READ)].astype(jnp.int32)
    owners = cycle_list[(cycle_place[:, None] + offsets[None, :]) % groups]
    slot_table = owners * P_DEV + (jnp.arange(READ, dtype=jnp.int32) // 2)[None, :]
    chosen = prompt_of[slot_table]
    rows_flat = jnp.repeat(chosen, HALF, axis=1)
    shuffle_keys = jax.random.split(jax.random.fold_in(key, 13), groups)
    shuffles = jax.vmap(lambda sub_key: jax.random.permutation(sub_key, ROWS))(shuffle_keys)
    shuffled = jnp.take_along_axis(rows_flat, shuffles, axis=1)
    return (slot_order, shuffled.reshape(-1).astype(jnp.int32))


def draw_prompt_slot(key, part):
    slot_order, shuffled = placement(key)
    return slot_order


def draw_sample_prompt(key, part):
    slot_order, shuffled = placement(key)
    return shuffled


def draw_prompt_key_cache(key, part):
    key = jax.random.fold_in(key, 5)
    unrotated_keys = jax.random.truncated_normal(key, -4.0, 4.0, (PROMPT_COUNT, PROMPT_SLOTS, KEY_HEADS * HEAD_SIZE), jnp.float32)
    return unrotated_keys.astype(jnp.bfloat16)


def shard_levels(own_key, shape, cuts, least, largest):
    def one(position, blocks):
        steps = jax.random.uniform(jax.random.fold_in(jax.random.fold_in(own_key, 6), position), (blocks,), jnp.float32, least / len(cuts), largest / len(cuts))
        return jnp.repeat(jnp.exp(steps), shape[position] // blocks).reshape((-1,) + (1,) * (len(shape) - position - 1))

    factor_of = one(*cuts[0])
    for cut in cuts[1:]:
        factor_of = factor_of * one(*cut)
    return factor_of


def split_up(number_of, total, bound, slope):
    weights = [(1 << 20) // math.isqrt(grade ** slope) + 1 for grade in range(2, number_of + 1)]
    surplus, holding = total - bound - (number_of - 1), [1] * (number_of - 1)
    while surplus > 0:
        movable = [i for i in range(number_of - 1) if holding[i] < bound]
        pool, left = sum([weights[i] for i in movable]), surplus
        for i in movable:
            addition = min(bound - holding[i], max(1, left * weights[i] // pool), surplus)
            holding[i] = holding[i] + addition
            surplus = surplus - addition
    return np.array([bound] + holding)


def uneven_parts(stream_key, amount, total, reach, skew):
    if amount == 2:
        one = jax.random.randint(stream_key, (), max(1, total - reach), min(reach, total - 1) + 1)
        return jnp.stack([one, total - one])
    lengths = jnp.asarray(split_up(amount, total, reach, skew), jnp.int32)
    twos = (amount - 1) // 2
    giver, sink = lengths[1:1 + 2 * twos:2], lengths[2:2 + 2 * twos:2]
    slack = jnp.minimum(giver - 1, reach - sink)
    passed = jax.random.randint(jax.random.fold_in(stream_key, 1), (twos,), 0, 1 << 20) % (slack + 1)
    lengths = lengths.at[1:1 + 2 * twos:2].set(giver - passed).at[2:2 + 2 * twos:2].set(sink + passed)
    return lengths[jax.random.permutation(jax.random.fold_in(stream_key, 2), amount)]


def centred(rng, dims, spread, limit, shards=(), kind=jnp.bfloat16):
    entries = jax.random.normal(rng, dims, jnp.float32) * spread
    if len(shards) > 0:
        entries = shard_levels(rng, dims, shards, -0.22, 0.18) * entries
    return jnp.clip(entries, min=-limit, max=limit).astype(kind)


def setup_inputs(seed: int = 0) -> dict:
    seeds = jax.random.split(jax.random.key(seed), 14)
    return {
        "inputs": centred(seeds[0], (STEPS, SAMPLES, MODEL_DIM), 1.0, 6.0, ((1, 32),)),
        "attn_gain": jnp.clip(jnp.exp(jax.random.uniform(seeds[1], (MODEL_DIM,), jnp.float32, math.log(0.5), math.log(2.0))), 0.5, 2.0),
        "w_query": centred(seeds[2], (MODEL_DIM, QUERY_HEADS * HEAD_SIZE), MODEL_DIM ** -0.5, 0.078125, ((1, 4),)),
        "key_matrix": centred(seeds[3], (MODEL_DIM, KEY_HEADS * HEAD_SIZE), MODEL_DIM ** -0.5, 0.078125, ((1, 4),)),
        "value_matrix": centred(seeds[4], (MODEL_DIM, KEY_HEADS * HEAD_SIZE), MODEL_DIM ** -0.5, 0.078125, ((1, 4),)),
        "q_gain": jnp.clip(jnp.exp(jax.random.uniform(seeds[5], (HEAD_SIZE,), jnp.float32, math.log(0.5), math.log(2.0))), 0.5, 2.0),
        "k_gain": jnp.clip(jnp.exp(jax.random.uniform(seeds[6], (HEAD_SIZE,), jnp.float32, math.log(0.5), math.log(2.0))), 0.5, 2.0),
        "w_out": centred(seeds[7], (QUERY_HEADS * HEAD_SIZE, MODEL_DIM), (HEAD_SIZE // 2) ** -0.5, 0.75, ((0, 4),)),
        "prompt_key_cache": draw_prompt_key_cache(jax.random.fold_in(seeds[13], 71), 0),
        "prompt_value_cache": centred(seeds[9], (PROMPT_COUNT, PROMPT_SLOTS, KEY_HEADS * HEAD_SIZE), 1.0, 6.0, ((0, 32), (2, 4))),
        "prompt_lengths": uneven_parts(seeds[10], PROMPT_COUNT, PROMPT_COUNT * PROMPT_SLOTS * 2 // 5, PROMPT_SLOTS, 2).astype(jnp.int32),
        "prompt_slot": draw_prompt_slot(jax.random.fold_in(seeds[13], 71), 0),
        "sample_prompt": draw_sample_prompt(jax.random.fold_in(seeds[13], 71), 0),
    }


epsilon = 1e-06
rope_base = 1000000.0

def rms_scale(values, gain_vector):
    return values * lax.rsqrt(lax.optimization_barrier(jnp.mean(values * values, axis=-1, keepdims=True)) + epsilon) * gain_vector

def rotate(values, positions):
    half_dim = values.shape[-1] // 2
    frequency = rope_base ** (-(jnp.arange(half_dim, dtype=jnp.float32) * 2.0 / values.shape[-1]))
    phase_angle = positions[..., None] * frequency
    cosine = jnp.cos(phase_angle)[..., None, :]
    sine_part = jnp.sin(phase_angle)[..., None, :]
    front_half = values[..., :half_dim]
    back_half = values[..., half_dim:]
    return jnp.concatenate([front_half * cosine - back_half * sine_part, back_half * cosine + front_half * sine_part], axis=-1)

def finish(summed, top_score, weight_sum, grouped_queries, new_keys, current_values, root_dim):
    step_total = grouped_queries.shape[0]
    fresh = jnp.einsum('trkgd,urkd->trkgu', grouped_queries.astype(jnp.float32), new_keys.astype(jnp.float32), precision=lax.Precision.HIGHEST) / root_dim
    causal = (jnp.arange(step_total)[None, :] <= jnp.arange(step_total)[:, None])[:, None, None, None, :]
    fresh_masked = jnp.where(causal, fresh, -1e+30)
    fresh_peak = lax.optimization_barrier(jnp.max(fresh_masked, axis=-1))
    fresh_weights = jnp.where(causal, jnp.exp(fresh_masked - fresh_peak[..., None]), 0.0)
    fresh_total = lax.optimization_barrier(jnp.sum(fresh_weights, axis=-1))
    fresh_sum = jnp.einsum('trkgu,urkd->trkgd', fresh_weights, current_values.astype(jnp.float32), precision=lax.Precision.HIGHEST)
    joint_peak = jnp.maximum(top_score, fresh_peak)
    early_scale = jnp.exp(top_score - joint_peak)
    late_scale = jnp.exp(fresh_peak - joint_peak)
    upper = summed * early_scale[..., None] + fresh_sum * late_scale[..., None]
    lower = weight_sum * early_scale + fresh_total * late_scale
    return (upper / lower[..., None]).astype(jnp.bfloat16)

def reference(inputs, attn_gain, w_query, key_matrix, value_matrix, q_gain, k_gain, w_out, prompt_key_cache, prompt_value_cache, prompt_lengths, prompt_slot, sample_prompt):
    step_total, sample_total, model_width = inputs.shape
    root_dim = math.sqrt(HEAD_SIZE)
    queries_per_key_head = QUERY_HEADS // KEY_HEADS
    row_length = prompt_lengths[sample_prompt].astype(jnp.int32)
    row_slot = prompt_slot[sample_prompt].astype(jnp.int32)
    positions = row_length[None, :].astype(jnp.float32) + jnp.arange(step_total, dtype=jnp.float32)[:, None]
    flat_rows = inputs.reshape(step_total * sample_total, model_width)
    normed_input = rms_scale(flat_rows.astype(jnp.float32), attn_gain).astype(jnp.bfloat16)
    query_raw = jnp.dot(normed_input, w_query, preferred_element_type=jnp.float32).reshape(step_total, sample_total, QUERY_HEADS, HEAD_SIZE)
    key_projected = jnp.dot(normed_input, key_matrix, preferred_element_type=jnp.float32).reshape(step_total, sample_total, KEY_HEADS, HEAD_SIZE)
    current_values = jnp.dot(normed_input, value_matrix, preferred_element_type=jnp.float32).astype(jnp.bfloat16).reshape(step_total, sample_total, KEY_HEADS, HEAD_SIZE)
    query_rows = rotate(rms_scale(query_raw, q_gain), positions).astype(jnp.bfloat16)
    new_keys = rotate(rms_scale(key_projected, k_gain), positions).astype(jnp.bfloat16)
    grouped_queries = query_rows.reshape(step_total, sample_total, KEY_HEADS, queries_per_key_head, HEAD_SIZE)

    def one_sample(packed):
        query_one, single_slot, limit_one = packed
        single_keys = lax.dynamic_index_in_dim(prompt_key_cache, single_slot, 0, keepdims=False).astype(jnp.float32).reshape(PROMPT_SLOTS, KEY_HEADS, HEAD_SIZE)
        single_values = lax.dynamic_index_in_dim(prompt_value_cache, single_slot, 0, keepdims=False).astype(jnp.float32).reshape(PROMPT_SLOTS, KEY_HEADS, HEAD_SIZE)
        scores = jnp.einsum('tkgd,lkd->tkgl', query_one.astype(jnp.float32), single_keys, precision=lax.Precision.HIGHEST) / root_dim
        valid = jnp.arange(PROMPT_SLOTS, dtype=jnp.int32) < limit_one
        masked = jnp.where(valid, scores, -1e+30)
        top_score = lax.optimization_barrier(jnp.max(masked, axis=-1))
        weights = jnp.where(valid, jnp.exp(masked - top_score[..., None]), 0.0).astype(jnp.bfloat16)
        weight_sum = lax.optimization_barrier(jnp.sum(weights.astype(jnp.float32), axis=-1))
        summed = jnp.einsum('tkgl,lkd->tkgd', weights.astype(jnp.float32), single_values, precision=lax.Precision.HIGHEST)
        return (summed, top_score, weight_sum)
    summed, top_score, weight_sum = lax.map(one_sample, (jnp.moveaxis(grouped_queries, 1, 0), row_slot, row_length))
    summed = jnp.moveaxis(summed, 0, 1)
    top_score = jnp.moveaxis(top_score, 0, 1)
    weight_sum = jnp.moveaxis(weight_sum, 0, 1)
    attended = finish(summed, top_score, weight_sum, grouped_queries, new_keys, current_values, root_dim)
    attended = attended.reshape(step_total * sample_total, QUERY_HEADS * HEAD_SIZE)
    output = jnp.dot(attended, w_out, preferred_element_type=jnp.float32).astype(jnp.bfloat16)
    return output.reshape(step_total, sample_total, model_width)
```

```python
import jax
import jax.numpy as jnp
import numpy as np
from jax import lax
from jax.experimental import pallas as pl
from jax.experimental.pallas import tpu as pltpu
from jax.sharding import PartitionSpec as P

MESH = pl.DeviceIdType.MESH
EPS = 1e-06
ROPE_BASE = 1000000.0
GROUPS = 32
TENSOR = 4
ROWS = 32
ITEMS = 4
HEADS = 8
DIM = 128
WIDTH = 5120
QCOLS = HEADS * DIM
SLOTS = 1024
FLAT = 2 * ROWS
QCHUNKS = 4
QCHUNK = QCOLS // QCHUNKS
SENDS = 2
SEND_COLS = QCOLS // SENDS
OUT_COLS = WIDTH // TENSOR
RET_ROWS = DIM + 16
SCALE = 1.0 / (DIM**0.5)
F32 = jnp.float32
BF16 = jnp.bfloat16


def dot_nt(a, b):
    return lax.dot_general(a, b, (((1,), (1,)), ((), ())), preferred_element_type=F32)


def dot_tn(a, b):
    return lax.dot_general(a, b, (((0,), (0,)), ((), ())), preferred_element_type=F32)


def split3(value):
    high = value.astype(BF16).astype(F32)
    rest = value - high
    middle = rest.astype(BF16).astype(F32)
    return high, middle, rest - middle


def kernel(
    len_ref, slot_ref, samp_ref, samp_v, gain, qg, kg, freq,
    x_hbm, wq_hbm, km_hbm, vm_hbm, wo_hbm, kc_hbm, vc_hbm,
    out_ref,
    x_v, wq_v, km_v, vm_v, wo_v, kc_v, vc_v, vt_v, xs_v, nm_v, q_s,
    send_q, recv_q, res_v, send_r, recv_r, att_v, ofr_v,
    sib_a, sib_b, rem_a, part_a, part_b, part_c,
    x_sem, wq_sem, mat_sem, wo_sem, cache_sem,
    qs_sem, qr_sem, rs_sem, rr_sem, ts_sem, tr_sem,
):
    me = lax.axis_index("group")
    rank = lax.axis_index("tensor")
    core = lax.rem(rank, 2)
    chip = rank // 2
    sibling = chip * 2 + (1 - core)
    remote = (1 - chip) * 2 + core
    far = (1 - chip) * 2 + (1 - core)

    x_copy = pltpu.make_async_copy(x_hbm, x_v, x_sem)
    x_copy.start()
    wq_copies = [
        pltpu.make_async_copy(
            wq_hbm.at[:, pl.ds(c * QCHUNK, QCHUNK)], wq_v.at[c], wq_sem.at[c]
        )
        for c in range(QCHUNKS)
    ]
    for copy in wq_copies:
        copy.start()
    mat_copies = [
        pltpu.make_async_copy(km_hbm, km_v, mat_sem.at[0]),
        pltpu.make_async_copy(vm_hbm, vm_v, mat_sem.at[1]),
    ]
    for copy in mat_copies:
        copy.start()

    barrier = pltpu.get_barrier_semaphore()

    def greet(k, carry):
        pl.semaphore_signal(
            barrier, inc=1, device_id={"group": lax.rem(me + k, GROUPS)}, device_id_type=MESH
        )
        return carry

    lax.fori_loop(1, GROUPS, greet, 0)
    for other in (sibling, remote):
        pl.semaphore_signal(barrier, inc=1, device_id={"tensor": other}, device_id_type=MESH)

    lane = lax.broadcasted_iota(jnp.int32, (1, FLAT), 1)
    sub = lax.broadcasted_iota(jnp.int32, (ROWS, FLAT), 0)
    key_lane = jnp.zeros((1, FLAT), jnp.int32)
    key_sub = jnp.zeros((ROWS, FLAT), jnp.int32)
    len_lane = jnp.zeros((1, FLAT), F32)
    row_of_lane = lax.rem(lane, ROWS)
    owners = []
    for r in range(ROWS):
        prompt = samp_ref[me * ROWS + r]
        owner = lax.shift_right_logical(slot_ref[prompt], 1)
        owners.append(owner)
        order_key = owner * ROWS + r
        key_lane = jnp.where(row_of_lane == r, order_key, key_lane)
        key_sub = jnp.where(sub == r, order_key, key_sub)
        len_lane = jnp.where(row_of_lane == r, len_ref[prompt].astype(F32), len_lane)
    item_owner = []
    floor = jnp.int32(-1)
    for _ in range(ITEMS):
        best = jnp.int32(GROUPS)
        for owner in owners:
            best = jnp.where((owner > floor) & (owner < best), owner, best)
        item_owner.append(best)
        floor = best

    place = jnp.sum((key_sub < key_lane).astype(jnp.int32), axis=0, keepdims=True)
    q_id = lax.broadcasted_iota(jnp.int32, (FLAT, FLAT), 0)
    c_id = lax.broadcasted_iota(jnp.int32, (FLAT, FLAT), 1)
    step_q = lax.rem(q_id // 8, 2)
    chosen = (step_q == c_id // ROWS) & ((q_id // 16) * 8 + lax.rem(q_id, 8) == place)
    sorter = jnp.where(chosen, 1.0, 0.0).astype(BF16)
    position = jnp.sum(jnp.where(chosen, len_lane, 0.0), axis=1, keepdims=True)
    position = position + step_q[:, :1].astype(F32)
    angle = position * freq[...]
    cosine = jnp.cos(angle)
    half = lax.broadcasted_iota(jnp.int32, (FLAT, DIM), 1) < DIM // 2
    sine = jnp.sin(angle)
    sine = jnp.where(half, -sine, sine)

    def head(values, gains):
        mean = jnp.mean(values * values, axis=-1, keepdims=True)
        scaled = values * lax.rsqrt(mean + EPS) * gains
        return (scaled * cosine + pltpu.roll(scaled, DIM // 2, 1) * sine).astype(BF16)

    x_copy.wait()
    total = jnp.zeros((FLAT, 1), F32)
    for c in range(5):
        cols = slice(c * 1024, (c + 1) * 1024)
        part = jnp.dot(sorter, x_v[:, cols], preferred_element_type=F32)
        xs_v[:, cols] = part
        total = total + jnp.sum(part * part, axis=1, keepdims=True)
    scale = lax.rsqrt(total * (1.0 / WIDTH) + EPS)
    for c in range(5):
        cols = slice(c * 1024, (c + 1) * 1024)
        nm_v[:, cols] = (xs_v[:, cols] * scale * gain[:, cols]).astype(BF16)

    group_id = (
        lax.broadcasted_iota(jnp.int32, (8, 128), 0) * 4
        + lax.broadcasted_iota(jnp.int32, (8, 128), 1) // ROWS
    )
    limits, readers = [], []
    for p in range(2):
        prompt = jnp.int32(0)
        for i in range(64):
            prompt = jnp.where(slot_ref[i] == me * 2 + p, jnp.int32(i), prompt)
        limits.append(len_ref[prompt])
        hit = samp_v[...] == prompt
        readers.append(jnp.min(jnp.where(hit, group_id, GROUPS - 1)))
        readers.append(jnp.max(jnp.where(hit, group_id, 0)))

    pl.semaphore_wait(barrier, GROUPS - 1 + 2)

    def item_for(dest):
        found = jnp.int32(0)
        for i in range(ITEMS - 1):
            found = found + (dest > item_owner[i]).astype(jnp.int32)
        return found

    for s in range(SENDS):
        for c in range(s * QCHUNKS // SENDS, (s + 1) * QCHUNKS // SENDS):
            wq_copies[c].wait()
            raw = jnp.dot(nm_v[...], wq_v[c], preferred_element_type=F32)
            for h in range(QCHUNK // DIM):
                turned = head(raw[:, h * DIM : (h + 1) * DIM], qg[...])
                at = c * QCHUNK + h * DIM
                q_s[:, :, at : at + DIM] = turned.reshape(ITEMS, 16, DIM)
        cols = slice(s * SEND_COLS, (s + 1) * SEND_COLS)
        recv_q[s, 0] = q_s[item_for(me), :, cols]

        def send(k, carry):
            dest = lax.rem(me + k, GROUPS)
            send_q[s, k] = q_s[item_for(dest), :, cols]
            pltpu.make_async_remote_copy(
                src_ref=send_q.at[s, k],
                dst_ref=recv_q.at[s, k],
                send_sem=qs_sem.at[s],
                recv_sem=qr_sem.at[s],
                device_id={"group": dest},
                device_id_type=MESH,
            ).start()
            return carry

        lax.fori_loop(1, GROUPS, send, 0)

    cache_copies = [
        pltpu.make_async_copy(kc_hbm, kc_v, cache_sem.at[0]),
        pltpu.make_async_copy(vc_hbm, vc_v, cache_sem.at[1]),
    ]
    for copy in cache_copies:
        copy.start()
    wo_copies = []
    for b, block in enumerate((far, remote, sibling, rank)):
        copy = pltpu.make_async_copy(
            wo_hbm.at[:, pl.ds(pl.multiple_of(block * OUT_COLS, OUT_COLS), OUT_COLS)],
            wo_v.at[b],
            wo_sem.at[b],
        )
        copy.start()
        wo_copies.append(copy)

    for copy in mat_copies:
        copy.wait()
    fresh_key = head(jnp.dot(nm_v[...], km_v[...], preferred_element_type=F32), kg[...])
    fresh_value = jnp.dot(nm_v[...], vm_v[...], preferred_element_type=F32).astype(BF16)
    q_all = jnp.concatenate(
        [q_s[i, :, h * DIM : (h + 1) * DIM] for i in range(ITEMS) for h in range(HEADS)], axis=0
    )
    cells = (FLAT, ITEMS * DIM)
    row_id = lax.broadcasted_iota(jnp.int32, cells, 0)
    col_id = lax.broadcasted_iota(jnp.int32, cells, 1)
    seen = (
        (row_id // 16 == col_id // DIM)
        & (lax.rem(row_id, 8) == lax.rem(col_id, 8))
        & (lax.rem(row_id // 8, 2) <= lax.rem(col_id // 8, 2))
    )
    fresh_score = jnp.where(seen, dot_nt(fresh_key, q_all) * SCALE, -1e30)
    fresh_peak = jnp.max(fresh_score, axis=0, keepdims=True)
    fresh_weight = jnp.where(seen, jnp.exp(fresh_score - fresh_peak), 0.0).astype(BF16)
    fresh_total = jnp.sum(fresh_weight.astype(F32), axis=0, keepdims=True)
    ofr_v[...] = dot_tn(fresh_value, fresh_weight)

    for copy in cache_copies:
        copy.wait()
    for p in range(2):
        vt_v[p] = vc_v[p].T

    for s in range(SENDS):
        pltpu.make_async_copy(
            send_q.at[s, pl.ds(1, GROUPS - 1)], recv_q.at[s, pl.ds(1, GROUPS - 1)], qr_sem.at[s]
        ).wait()

    key_id = lax.broadcasted_iota(jnp.int32, (SLOTS, 2 * DIM), 0)
    stat_id = lax.broadcasted_iota(jnp.int32, (16, 2 * DIM), 0)
    for p in range(2):
        blocks = []
        for i in range(2):
            at = lax.rem(me - readers[2 * p + i] + GROUPS, GROUPS)
            for s in range(SENDS):
                got = recv_q[s, at]
                blocks += [got[:, h * DIM : (h + 1) * DIM] for h in range(HEADS // SENDS)]
        queries = jnp.concatenate(blocks, axis=0)
        valid = key_id < limits[p]
        score = jnp.where(valid, dot_nt(kc_v[p], queries) * SCALE, -1e30)
        peak = jnp.max(score, axis=0, keepdims=True)
        weight = jnp.where(valid, jnp.exp(score - peak), 0.0).astype(BF16)
        amount = jnp.sum(weight.astype(F32), axis=0, keepdims=True)
        summed = jnp.dot(vt_v[p], weight, preferred_element_type=F32).astype(BF16)
        stats = jnp.zeros((16, 2 * DIM), F32)
        for n, part in enumerate(split3(peak) + split3(amount)):
            stats = jnp.where(stat_id == n, part, stats)
        stats = stats.astype(BF16)
        for i in range(2):
            cols = slice(i * DIM, (i + 1) * DIM)
            res_v[2 * p + i, :DIM] = summed[:, cols]
            res_v[2 * p + i, DIM:] = stats[:, cols]

    def result_for(dest):
        found = jnp.int32(0)
        for i in range(1, ITEMS):
            found = jnp.where(dest == readers[i], jnp.int32(i), found)
        return found

    recv_r[0] = res_v[result_for(me)]

    def give_back(k, carry):
        dest = lax.rem(me + k, GROUPS)
        send_r[k] = res_v[result_for(dest)]
        pltpu.make_async_remote_copy(
            src_ref=send_r.at[k],
            dst_ref=recv_r.at[k],
            send_sem=rs_sem,
            recv_sem=rr_sem,
            device_id={"group": dest},
            device_id_type=MESH,
        ).start()
        return carry

    lax.fori_loop(1, GROUPS, give_back, 0)
    pltpu.make_async_copy(
        send_r.at[pl.ds(1, GROUPS - 1)], recv_r.at[pl.ds(1, GROUPS - 1)], rr_sem
    ).wait()

    for i in range(ITEMS):
        got = recv_r[lax.rem(me - item_owner[i] + GROUPS, GROUPS)]
        cols = slice(i * DIM, (i + 1) * DIM)
        stats = got[DIM:].astype(F32)
        peak = stats[0:1] + stats[1:2] + stats[2:3]
        amount = stats[3:4] + stats[4:5] + stats[5:6]
        own_peak = fresh_peak[:, cols]
        joint = jnp.maximum(peak, own_peak)
        early = jnp.exp(peak - joint)
        late = jnp.exp(own_peak - joint)
        upper = got[:DIM].astype(F32) * early + ofr_v[:, cols] * late
        lower = amount * early + fresh_total[:, cols] * late
        done = (upper / lower).T.astype(BF16)
        for h in range(HEADS):
            att_v[i * 16 : (i + 1) * 16, h * DIM : (h + 1) * DIM] = done[h * 16 : (h + 1) * 16]
    attended = dot_tn(sorter, att_v[...]).astype(BF16)

    def pass_on(n, source, target, device):
        return pltpu.make_async_remote_copy(
            src_ref=source,
            dst_ref=target,
            send_sem=ts_sem.at[n],
            recv_sem=tr_sem.at[n],
            device_id={"tensor": device},
            device_id_type=MESH,
        )

    wo_copies[0].wait()
    part_a[...] = jnp.dot(attended, wo_v[0], preferred_element_type=F32).astype(BF16)
    first = pass_on(0, part_a, sib_a, sibling)
    first.start()
    wo_copies[1].wait()
    mine = jnp.dot(attended, wo_v[1], preferred_element_type=F32)
    first.wait_recv()
    part_b[...] = (mine + sib_a[...].astype(F32)).astype(BF16)
    second = pass_on(1, part_b, rem_a, remote)
    second.start()
    wo_copies[2].wait()
    part_c[...] = jnp.dot(attended, wo_v[2], preferred_element_type=F32).astype(BF16)
    third = pass_on(2, part_c, sib_b, sibling)
    third.start()
    wo_copies[3].wait()
    mine = jnp.dot(attended, wo_v[3], preferred_element_type=F32)
    third.wait_recv()
    mine = mine + sib_b[...].astype(F32)
    second.wait_recv()
    out_ref[...] = (mine + rem_a[...].astype(F32)).astype(BF16)

    for copy in (first, second, third):
        copy.wait_send()
    for s in range(SENDS):
        pltpu.make_async_copy(
            send_q.at[s, pl.ds(1, GROUPS - 1)], recv_q.at[s, pl.ds(1, GROUPS - 1)], qs_sem.at[s]
        ).wait()
    pltpu.make_async_copy(
        send_r.at[pl.ds(1, GROUPS - 1)], recv_r.at[pl.ds(1, GROUPS - 1)], rs_sem
    ).wait()


def shards(
    inputs,
    attn_gain,
    w_query,
    key_matrix,
    value_matrix,
    q_gain,
    k_gain,
    w_out,
    prompt_key_cache,
    prompt_value_cache,
    prompt_lengths,
    prompt_slot,
    sample_prompt,
):
    half = np.arange(DIM // 2, dtype=np.float64)
    frequency = ROPE_BASE ** (-(half * 2.0 / DIM))
    frequency = jnp.asarray(np.concatenate([frequency, frequency])[None, :], F32)
    smem = pl.BlockSpec(memory_space=pltpu.SMEM)
    vmem = pl.BlockSpec(memory_space=pltpu.VMEM)
    anywhere = pl.BlockSpec(memory_space=pl.ANY)
    dma = pltpu.SemaphoreType.DMA
    out = pl.pallas_call(
        kernel,
        out_shape=jax.ShapeDtypeStruct((FLAT, OUT_COLS), BF16),
        in_specs=[smem] * 3 + [vmem] * 5 + [anywhere] * 7,
        out_specs=vmem,
        scratch_shapes=[
            pltpu.VMEM((FLAT, WIDTH), BF16),
            pltpu.VMEM((QCHUNKS, WIDTH, QCHUNK), BF16),
            pltpu.VMEM((WIDTH, DIM), BF16),
            pltpu.VMEM((WIDTH, DIM), BF16),
            pltpu.VMEM((TENSOR, QCOLS, OUT_COLS), BF16),
            pltpu.VMEM((2, SLOTS, DIM), BF16),
            pltpu.VMEM((2, SLOTS, DIM), BF16),
            pltpu.VMEM((2, DIM, SLOTS), BF16),
            pltpu.VMEM((FLAT, WIDTH), F32),
            pltpu.VMEM((FLAT, WIDTH), BF16),
            pltpu.VMEM((ITEMS, 16, QCOLS), BF16),
            pltpu.VMEM((SENDS, GROUPS, 16, SEND_COLS), BF16),
            pltpu.VMEM((SENDS, GROUPS, 16, SEND_COLS), BF16),
            pltpu.VMEM((ITEMS, RET_ROWS, DIM), BF16),
            pltpu.VMEM((GROUPS, RET_ROWS, DIM), BF16),
            pltpu.VMEM((GROUPS, RET_ROWS, DIM), BF16),
            pltpu.VMEM((FLAT, QCOLS), BF16),
            pltpu.VMEM((DIM, ITEMS * DIM), F32),
            pltpu.VMEM((FLAT, OUT_COLS), BF16),
            pltpu.VMEM((FLAT, OUT_COLS), BF16),
            pltpu.VMEM((FLAT, OUT_COLS), BF16),
            pltpu.VMEM((FLAT, OUT_COLS), BF16),
            pltpu.VMEM((FLAT, OUT_COLS), BF16),
            pltpu.VMEM((FLAT, OUT_COLS), BF16),
            dma,
            dma((QCHUNKS,)),
            dma((2,)),
            dma((TENSOR,)),
            dma((2,)),
            dma((SENDS,)),
            dma((SENDS,)),
            dma,
            dma,
            dma((3,)),
            dma((3,)),
        ],
        compiler_params=pltpu.CompilerParams(
            collective_id=0, has_side_effects=True, vmem_limit_bytes=56 * 1024 * 1024
        ),
    )(
        prompt_lengths,
        prompt_slot,
        sample_prompt,
        sample_prompt.reshape(8, 128),
        attn_gain.reshape(1, WIDTH),
        q_gain.reshape(1, DIM),
        k_gain.reshape(1, DIM),
        frequency,
        inputs.reshape(FLAT, WIDTH),
        w_query,
        key_matrix,
        value_matrix,
        w_out,
        prompt_key_cache,
        prompt_value_cache,
    )
    return out.reshape(2, ROWS, OUT_COLS)


def solution(mesh):
    in_specs = (
        P(None, "group", None),
        P(),
        P(None, "tensor"),
        P(None, "tensor"),
        P(None, "tensor"),
        P(),
        P(),
        P("tensor", None),
        P("group", None, "tensor"),
        P("group", None, "tensor"),
        P(),
        P(),
        P(),
    )
    out_specs = P(None, "group", "tensor")
    return jax.shard_map(shards, mesh=mesh, in_specs=in_specs, out_specs=out_specs, check_vma=False)
```

```python
import jax
import jax.numpy as jnp
import numpy as np
from jax import lax
from jax.experimental import pallas as pl
from jax.experimental.pallas import tpu as pltpu
from jax.sharding import PartitionSpec as P

MESH = pl.DeviceIdType.MESH
EPS = 1e-06
ROPE_BASE = 1000000.0
GROUPS = 32
TENSOR = 4
ROWS = 32
ITEMS = 4
HEADS = 8
DIM = 128
WIDTH = 5120
QCOLS = HEADS * DIM
SLOTS = 1024
FLAT = 2 * ROWS
DEPTH = 4
SENDS = 2
SEND_COLS = QCOLS // SENDS
OUT_COLS = WIDTH // TENSOR
HALF_HEADS = HEADS // SENDS
HALF_ROWS = HALF_HEADS * 16
PIECES = 4
PIECE = WIDTH // PIECES
OUT_HALF = OUT_COLS // 2
SCALE = 1.0 / (DIM**0.5)
F32 = jnp.float32
BF16 = jnp.bfloat16


def dot_nt(a, b):
    return lax.dot_general(a, b, (((1,), (1,)), ((), ())), preferred_element_type=F32)


def dot_tn(a, b):
    return lax.dot_general(a, b, (((0,), (0,)), ((), ())), preferred_element_type=F32)


def kernel(
    len_ref, slot_ref, samp_ref, samp_v, gain, qg, kg, freq,
    x_hbm, wq_hbm, km_hbm, vm_hbm, wo_hbm, kc_hbm, vc_hbm,
    out_ref,
    x_v, wq_v, km_v, vm_v, wo_v, kc_v, vc_v, vt_v, xs_v, nm_v, q_s,
    send_q, recv_q0, recv_q1, res_v, stat_v, send_r, recv_r0, recv_r1, send_t, recv_t0, recv_t1, att_v, ofr_v, acc_v,
    sib_a, sib_b, rem_a, part_a, part_b, part_c, own_v,
    x_sem, wq_sem, mat_sem, wo_sem, cache_sem,
    qs_sem, qr_sem, rs_sem, rr_sem, ss_sem, sr_sem, ts_sem, tr_sem,
):
    recv_q, recv_r, recv_t = (recv_q0, recv_q1), (recv_r0, recv_r1), (recv_t0, recv_t1)
    me = lax.axis_index("group")
    rank = lax.axis_index("tensor")
    core = lax.rem(rank, 2)
    chip = rank // 2
    sibling = chip * 2 + (1 - core)
    remote = (1 - chip) * 2 + core
    far = (1 - chip) * 2 + (1 - core)

    x_copy = pltpu.make_async_copy(x_hbm, x_v, x_sem)
    x_copy.start()
    wq_copies = [
        pltpu.make_async_copy(
            wq_hbm.at[pl.ds(n * PIECE, PIECE), pl.ds(s * SEND_COLS, SEND_COLS)],
            wq_v.at[s, pl.ds(n * PIECE, PIECE)],
            wq_sem.at[s, n],
        )
        for s in range(SENDS)
        for n in range(PIECES)
    ]
    for copy in wq_copies[:DEPTH]:
        copy.start()
    mat_copies = [
        pltpu.make_async_copy(km_hbm, km_v, mat_sem.at[0]),
        pltpu.make_async_copy(vm_hbm, vm_v, mat_sem.at[1]),
    ]

    barrier = pltpu.get_barrier_semaphore()

    def greet(k, carry):
        pl.semaphore_signal(
            barrier, inc=1, device_id={"group": lax.rem(me + k, GROUPS)}, device_id_type=MESH
        )
        return carry

    lax.fori_loop(1, GROUPS, greet, 0)
    for other in (sibling, remote):
        pl.semaphore_signal(barrier, inc=1, device_id={"tensor": other}, device_id_type=MESH)

    lane = lax.broadcasted_iota(jnp.int32, (1, FLAT), 1)
    sub = lax.broadcasted_iota(jnp.int32, (ROWS, FLAT), 0)
    key_lane = jnp.zeros((1, FLAT), jnp.int32)
    key_sub = jnp.zeros((ROWS, FLAT), jnp.int32)
    len_lane = jnp.zeros((1, FLAT), F32)
    row_of_lane = lax.rem(lane, ROWS)
    owners = []
    for r in range(ROWS):
        prompt = samp_ref[me * ROWS + r]
        owner = lax.shift_right_logical(slot_ref[prompt], 1)
        owners.append(owner)
        order_key = owner * ROWS + r
        key_lane = jnp.where(row_of_lane == r, order_key, key_lane)
        key_sub = jnp.where(sub == r, order_key, key_sub)
        len_lane = jnp.where(row_of_lane == r, len_ref[prompt].astype(F32), len_lane)
    item_owner = []
    floor = jnp.int32(-1)
    for _ in range(ITEMS):
        best = jnp.int32(GROUPS)
        for owner in owners:
            best = jnp.where((owner > floor) & (owner < best), owner, best)
        item_owner.append(best)
        floor = best

    place = jnp.sum((key_sub < key_lane).astype(jnp.int32), axis=0, keepdims=True)
    q_id = lax.broadcasted_iota(jnp.int32, (FLAT, FLAT), 0)
    c_id = lax.broadcasted_iota(jnp.int32, (FLAT, FLAT), 1)
    step_q = lax.rem(q_id // 8, 2)
    chosen = (step_q == c_id // ROWS) & ((q_id // 16) * 8 + lax.rem(q_id, 8) == place)
    sorter = jnp.where(chosen, 1.0, 0.0).astype(BF16)
    position = jnp.sum(jnp.where(chosen, len_lane, 0.0), axis=1, keepdims=True)
    position = position + step_q[:, :1].astype(F32)
    angle = position * freq[...]
    cosine = jnp.cos(angle)
    half = lax.broadcasted_iota(jnp.int32, (FLAT, DIM), 1) < DIM // 2
    sine = jnp.sin(angle)
    sine = jnp.where(half, -sine, sine)

    def head(values, gains):
        mean = jnp.mean(values * values, axis=-1, keepdims=True)
        scaled = values * lax.rsqrt(mean + EPS) * gains
        return (scaled * cosine + pltpu.roll(scaled, DIM // 2, 1) * sine).astype(BF16)

    x_copy.wait()
    total = jnp.zeros((FLAT, 1), F32)
    for c in range(5):
        cols = slice(c * 1024, (c + 1) * 1024)
        part = jnp.dot(sorter, x_v[:, cols], preferred_element_type=F32)
        xs_v[:, cols] = part
        total = total + jnp.sum(part * part, axis=1, keepdims=True)
    scale = lax.rsqrt(total * (1.0 / WIDTH) + EPS)
    for c in range(5):
        cols = slice(c * 1024, (c + 1) * 1024)
        nm_v[:, cols] = (xs_v[:, cols] * scale * gain[:, cols]).astype(BF16)

    group_id = (
        lax.broadcasted_iota(jnp.int32, (8, 128), 0) * 4
        + lax.broadcasted_iota(jnp.int32, (8, 128), 1) // ROWS
    )
    limits, readers = [], []
    for p in range(2):
        prompt = jnp.int32(0)
        for i in range(64):
            prompt = jnp.where(slot_ref[i] == me * 2 + p, jnp.int32(i), prompt)
        limits.append(len_ref[prompt])
        hit = samp_v[...] == prompt
        readers.append(jnp.min(jnp.where(hit, group_id, GROUPS - 1)))
        readers.append(jnp.max(jnp.where(hit, group_id, 0)))


    def shuffled(n):
        return lax.rem(n * 12, GROUPS - 1) + 1

    def item_for(dest):
        found = jnp.int32(0)
        for i in range(ITEMS - 1):
            found = found + (dest > item_owner[i]).astype(jnp.int32)
        return found

    for s in range(SENDS):
        raw = None
        for n in range(PIECES):
            at = s * PIECES + n
            wq_copies[at].wait()
            if at + DEPTH < len(wq_copies):
                wq_copies[at + DEPTH].start()
            elif at + DEPTH == len(wq_copies):
                for copy in mat_copies:
                    copy.start()
            rows = slice(n * PIECE, (n + 1) * PIECE)
            part = jnp.dot(nm_v[:, rows], wq_v[s, rows], preferred_element_type=F32)
            raw = part if raw is None else raw + part
        for h in range(HALF_HEADS):
            turned = head(raw[:, h * DIM : (h + 1) * DIM], qg[...])
            at = (s * HALF_HEADS + h) * DIM
            q_s[:, :, at : at + DIM] = turned.reshape(ITEMS, 16, DIM)
        if s == 0:
            pl.semaphore_wait(barrier, GROUPS - 1 + 2)
        cols = slice(s * SEND_COLS, (s + 1) * SEND_COLS)
        recv_q[s][0] = q_s[item_for(me), :, cols]

        def send(n, carry):
            k = shuffled(n)
            dest = lax.rem(me + k, GROUPS)
            send_q[s, k] = q_s[item_for(dest), :, cols]
            pltpu.make_async_remote_copy(
                src_ref=send_q.at[s, k],
                dst_ref=recv_q[s].at[k],
                send_sem=qs_sem.at[s],
                recv_sem=qr_sem.at[s],
                device_id={"group": dest},
                device_id_type=MESH,
            ).start()
            return carry

        lax.fori_loop(0, GROUPS - 1, send, 0)

    cache_copies = [
        pltpu.make_async_copy(kc_hbm, kc_v, cache_sem.at[0]),
        pltpu.make_async_copy(vc_hbm, vc_v, cache_sem.at[1]),
    ]
    for copy in cache_copies:
        copy.start()
    wo_copies = []
    for b, block in enumerate((far, remote, sibling, rank)):
        copy = pltpu.make_async_copy(
            wo_hbm.at[:, pl.ds(pl.multiple_of(block * OUT_COLS, OUT_COLS), OUT_COLS)],
            wo_v.at[b],
            wo_sem.at[b],
        )
        copy.start()
        wo_copies.append(copy)

    for copy in mat_copies:
        copy.wait()
    fresh_key = head(jnp.dot(nm_v[...], km_v[...], preferred_element_type=F32), kg[...])
    fresh_value = jnp.dot(nm_v[...], vm_v[...], preferred_element_type=F32).astype(BF16)
    q_all = jnp.concatenate(
        [
            q_s[i, :, h * DIM : (h + 1) * DIM]
            for s in range(SENDS)
            for i in range(ITEMS)
            for h in range(s * HALF_HEADS, (s + 1) * HALF_HEADS)
        ],
        axis=0,
    )
    cells = (FLAT, ITEMS * DIM)
    row_id = lax.broadcasted_iota(jnp.int32, cells, 0)
    col_id = lax.broadcasted_iota(jnp.int32, cells, 1)
    seen = (
        (row_id // 16 == lax.rem(col_id // HALF_ROWS, ITEMS))
        & (lax.rem(row_id, 8) == lax.rem(col_id, 8))
        & (lax.rem(row_id // 8, 2) <= lax.rem(col_id // 8, 2))
    )
    fresh_score = jnp.where(seen, dot_nt(fresh_key, q_all) * SCALE, -1e30)
    fresh_peak = jnp.max(fresh_score, axis=0, keepdims=True)
    fresh_weight = jnp.where(seen, jnp.exp(fresh_score - fresh_peak), 0.0).astype(BF16)
    fresh_total = jnp.sum(fresh_weight.astype(F32), axis=0, keepdims=True)
    ofr_v[...] = dot_tn(fresh_weight, fresh_value)

    for copy in cache_copies:
        copy.wait()
    for p in range(2):
        vt_v[p] = vc_v[p].T

    key_id = lax.broadcasted_iota(jnp.int32, (SLOTS, DIM), 0)
    first_half = lax.broadcasted_iota(jnp.int32, (1, DIM), 1) < HALF_ROWS

    def result_for(dest):
        found = jnp.int32(0)
        for i in range(1, ITEMS):
            found = jnp.where(dest == readers[i], jnp.int32(i), found)
        return found

    for s in range(SENDS):
        pltpu.make_async_copy(
            send_q.at[s, pl.ds(1, GROUPS - 1)], recv_q[s].at[pl.ds(1, GROUPS - 1)], qr_sem.at[s]
        ).wait()
        for p in range(2):
            blocks = []
            for i in range(2):
                got = recv_q[s][lax.rem(me - readers[2 * p + i] + GROUPS, GROUPS)]
                blocks += [got[:, h * DIM : (h + 1) * DIM] for h in range(HALF_HEADS)]
            queries = jnp.concatenate(blocks, axis=0)
            valid = key_id < limits[p]
            score = jnp.where(valid, dot_nt(kc_v[p], queries) * SCALE, -1e30)
            peak = jnp.max(score, axis=0, keepdims=True)
            weight = jnp.where(valid, jnp.exp(score - peak), 0.0).astype(BF16)
            amount = jnp.sum(weight.astype(F32), axis=0, keepdims=True)
            summed = jnp.dot(vt_v[p], weight, preferred_element_type=F32).T.astype(BF16)
            for i in range(2):
                res_v[s, 2 * p + i] = summed[i * HALF_ROWS : (i + 1) * HALF_ROWS]
            peak_turned = pltpu.roll(peak, HALF_ROWS, 1)
            amount_turned = pltpu.roll(amount, HALF_ROWS, 1)
            stat_v[s, 2 * p] = jnp.where(first_half, peak, amount_turned)
            stat_v[s, 2 * p + 1] = jnp.where(first_half, peak_turned, amount)

        recv_r[s][0] = res_v[s, result_for(me)]
        recv_t[s][0] = stat_v[s, result_for(me)]

        def give_back(n, carry):
            k = shuffled(n)
            dest = lax.rem(me + k, GROUPS)
            found = result_for(dest)
            send_r[s, k] = res_v[s, found]
            send_t[s, k] = stat_v[s, found]
            pltpu.make_async_remote_copy(
                src_ref=send_t.at[s, k],
                dst_ref=recv_t[s].at[k],
                send_sem=ss_sem.at[s],
                recv_sem=sr_sem.at[s],
                device_id={"group": dest},
                device_id_type=MESH,
            ).start()
            pltpu.make_async_remote_copy(
                src_ref=send_r.at[s, k],
                dst_ref=recv_r[s].at[k],
                send_sem=rs_sem.at[s],
                recv_sem=rr_sem.at[s],
                device_id={"group": dest},
                device_id_type=MESH,
            ).start()
            return carry

        lax.fori_loop(0, GROUPS - 1, give_back, 0)

    def wait_all(sent, got_back, sem, s):
        pltpu.make_async_copy(
            sent.at[s, pl.ds(1, GROUPS - 1)], got_back[s].at[pl.ds(1, GROUPS - 1)], sem.at[s]
        ).wait()

    places = [lax.rem(me - owner + GROUPS, GROUPS) for owner in item_owner]
    factor_id = lax.broadcasted_iota(jnp.int32, (8, ITEMS * HALF_ROWS), 0)

    def merge(s):
        wait_all(send_t, recv_t, sr_sem, s)
        wait_all(send_r, recv_r, rr_sem, s)
        stats = [recv_t[s][at] for at in places]
        peak = jnp.concatenate([stat[:, :HALF_ROWS] for stat in stats], axis=1)
        amount = jnp.concatenate([stat[:, HALF_ROWS:] for stat in stats], axis=1)
        cols = slice(s * ITEMS * HALF_ROWS, (s + 1) * ITEMS * HALF_ROWS)
        own_peak = fresh_peak[:, cols]
        joint = jnp.maximum(peak, own_peak)
        early = jnp.exp(peak - joint)
        late = jnp.exp(own_peak - joint)
        lower = amount * early + fresh_total[:, cols] * late
        factors = jnp.where(factor_id == 0, early / lower, late / lower).T
        for i in range(ITEMS):
            got = recv_r[s][places[i]].astype(F32)
            low = i * HALF_ROWS
            at = (s * ITEMS + i) * HALF_ROWS
            done = got * factors[low : low + HALF_ROWS, 0:1]
            done = done + ofr_v[at : at + HALF_ROWS] * factors[low : low + HALF_ROWS, 1:2]
            done = done.astype(BF16)
            for h in range(HALF_HEADS):
                col = h * DIM
                att_v[s, i * 16 : (i + 1) * 16, col : col + DIM] = done[h * 16 : (h + 1) * 16]
        return dot_tn(sorter, att_v[s]).astype(BF16)

    attended = merge(0)
    for block in range(TENSOR):
        wo_copies[block].wait()
        acc_v[block] = jnp.dot(
            attended, wo_v[block, : HALF_HEADS * DIM], preferred_element_type=F32
        )
    attended = merge(1)
    def pass_on(n, source, target, device):
        return pltpu.make_async_remote_copy(
            src_ref=source,
            dst_ref=target,
            send_sem=ts_sem.at[n],
            recv_sem=tr_sem.at[n],
            device_id={"tensor": device},
            device_id_type=MESH,
        )

    def project(block, half):
        cols = slice(half * OUT_HALF, (half + 1) * OUT_HALF)
        last = wo_v[block, HALF_HEADS * DIM :, cols]
        return acc_v[block, :, cols] + jnp.dot(attended, last, preferred_element_type=F32)

    halves = range(2)
    first, second, third = [], [], []
    for half in halves:
        part_a[half] = project(0, half).astype(BF16)
        first.append(pass_on(half, part_a.at[half], sib_a.at[half], sibling))
        first[half].start()
    for half in halves:
        mine = project(1, half)
        first[half].wait_recv()
        part_b[half] = (mine + sib_a[half].astype(F32)).astype(BF16)
        second.append(pass_on(2 + half, part_b.at[half], rem_a.at[half], remote))
        second[half].start()
    for half in halves:
        part_c[half] = project(2, half).astype(BF16)
        third.append(pass_on(4 + half, part_c.at[half], sib_b.at[half], sibling))
        third[half].start()
    for half in halves:
        mine = project(3, half)
        third[half].wait_recv()
        own_v[half] = mine + sib_b[half].astype(F32)
    for half in halves:
        second[half].wait_recv()
        cols = slice(half * OUT_HALF, (half + 1) * OUT_HALF)
        out_ref[:, cols] = (own_v[half] + rem_a[half].astype(F32)).astype(BF16)

    for copy in first + second + third:
        copy.wait_send()
    for s in range(SENDS):
        pltpu.make_async_copy(
            send_q.at[s, pl.ds(1, GROUPS - 1)], recv_q[s].at[pl.ds(1, GROUPS - 1)], qs_sem.at[s]
        ).wait()
    for s in range(SENDS):
        wait_all(send_r, recv_r, rs_sem, s)
        wait_all(send_t, recv_t, ss_sem, s)


def shards(
    inputs,
    attn_gain,
    w_query,
    key_matrix,
    value_matrix,
    q_gain,
    k_gain,
    w_out,
    prompt_key_cache,
    prompt_value_cache,
    prompt_lengths,
    prompt_slot,
    sample_prompt,
):
    half = np.arange(DIM // 2, dtype=np.float64)
    frequency = ROPE_BASE ** (-(half * 2.0 / DIM))
    frequency = jnp.asarray(np.concatenate([frequency, frequency])[None, :], F32)
    smem = pl.BlockSpec(memory_space=pltpu.SMEM)
    vmem = pl.BlockSpec(memory_space=pltpu.VMEM)
    anywhere = pl.BlockSpec(memory_space=pl.ANY)
    dma = pltpu.SemaphoreType.DMA
    out = pl.pallas_call(
        kernel,
        out_shape=jax.ShapeDtypeStruct((FLAT, OUT_COLS), BF16),
        in_specs=[smem] * 3 + [vmem] * 5 + [anywhere] * 7,
        out_specs=vmem,
        scratch_shapes=[
            pltpu.VMEM((FLAT, WIDTH), BF16),
            pltpu.VMEM((SENDS, WIDTH, SEND_COLS), BF16),
            pltpu.VMEM((WIDTH, DIM), BF16),
            pltpu.VMEM((WIDTH, DIM), BF16),
            pltpu.VMEM((TENSOR, QCOLS, OUT_COLS), BF16),
            pltpu.VMEM((2, SLOTS, DIM), BF16),
            pltpu.VMEM((2, SLOTS, DIM), BF16),
            pltpu.VMEM((2, DIM, SLOTS), BF16),
            pltpu.VMEM((FLAT, WIDTH), F32),
            pltpu.VMEM((FLAT, WIDTH), BF16),
            pltpu.VMEM((ITEMS, 16, QCOLS), BF16),
            pltpu.VMEM((SENDS, GROUPS, 16, SEND_COLS), BF16),
            pltpu.VMEM((GROUPS, 16, SEND_COLS), BF16),
            pltpu.VMEM((GROUPS, 16, SEND_COLS), BF16),
            pltpu.VMEM((SENDS, ITEMS, HALF_ROWS, DIM), BF16),
            pltpu.VMEM((SENDS, ITEMS, 1, DIM), F32),
            pltpu.VMEM((SENDS, GROUPS, HALF_ROWS, DIM), BF16),
            pltpu.VMEM((GROUPS, HALF_ROWS, DIM), BF16),
            pltpu.VMEM((GROUPS, HALF_ROWS, DIM), BF16),
            pltpu.VMEM((SENDS, GROUPS, 1, DIM), F32),
            pltpu.VMEM((GROUPS, 1, DIM), F32),
            pltpu.VMEM((GROUPS, 1, DIM), F32),
            pltpu.VMEM((SENDS, FLAT, SEND_COLS), BF16),
            pltpu.VMEM((ITEMS * DIM, DIM), F32),
            pltpu.VMEM((TENSOR, FLAT, OUT_COLS), F32),
            pltpu.VMEM((2, FLAT, OUT_HALF), BF16),
            pltpu.VMEM((2, FLAT, OUT_HALF), BF16),
            pltpu.VMEM((2, FLAT, OUT_HALF), BF16),
            pltpu.VMEM((2, FLAT, OUT_HALF), BF16),
            pltpu.VMEM((2, FLAT, OUT_HALF), BF16),
            pltpu.VMEM((2, FLAT, OUT_HALF), BF16),
            pltpu.VMEM((2, FLAT, OUT_HALF), F32),
            dma,
            dma((SENDS, PIECES)),
            dma((2,)),
            dma((TENSOR,)),
            dma((2,)),
            dma((SENDS,)),
            dma((SENDS,)),
            dma((SENDS,)),
            dma((SENDS,)),
            dma((SENDS,)),
            dma((SENDS,)),
            dma((6,)),
            dma((6,)),
        ],
        compiler_params=pltpu.CompilerParams(
            collective_id=0, has_side_effects=True, vmem_limit_bytes=56 * 1024 * 1024
        ),
    )(
        prompt_lengths,
        prompt_slot,
        sample_prompt,
        sample_prompt.reshape(8, 128),
        attn_gain.reshape(1, WIDTH),
        q_gain.reshape(1, DIM),
        k_gain.reshape(1, DIM),
        frequency,
        inputs.reshape(FLAT, WIDTH),
        w_query,
        key_matrix,
        value_matrix,
        w_out,
        prompt_key_cache,
        prompt_value_cache,
    )
    return out.reshape(2, ROWS, OUT_COLS)


def solution(mesh):
    in_specs = (
        P(None, "group", None),
        P(),
        P(None, "tensor"),
        P(None, "tensor"),
        P(None, "tensor"),
        P(),
        P(),
        P("tensor", None),
        P("group", None, "tensor"),
        P("group", None, "tensor"),
        P(),
        P(),
        P(),
    )
    out_specs = P(None, "group", "tensor")
    return jax.shard_map(shards, mesh=mesh, in_specs=in_specs, out_specs=out_specs, check_vma=False)
```

```python
import jax
import jax.numpy as jnp
import numpy as np
from jax import lax
from jax.experimental import pallas as pl
from jax.experimental.pallas import tpu as pltpu
from jax.sharding import PartitionSpec as P

MESH = pl.DeviceIdType.MESH
EPS = 1e-06
ROPE_BASE = 1000000.0
GROUPS = 32
TENSOR = 4
ROWS = 32
ITEMS = 4
HEADS = 8
DIM = 128
WIDTH = 5120
QCOLS = HEADS * DIM
SLOTS = 1024
FLAT = 2 * ROWS
DEPTH = 4
SENDS = 2
SEND_COLS = QCOLS // SENDS
OUT_COLS = WIDTH // TENSOR
HALF_HEADS = HEADS // SENDS
HALF_ROWS = HALF_HEADS * 16
PIECES = 4
PIECE = WIDTH // PIECES
STEP_ROWS = HALF_HEADS * 8
SCALE = 1.0 / (DIM**0.5)
F32 = jnp.float32
BF16 = jnp.bfloat16


def dot_nt(a, b):
    return lax.dot_general(a, b, (((1,), (1,)), ((), ())), preferred_element_type=F32)


def dot_tn(a, b):
    return lax.dot_general(a, b, (((0,), (0,)), ((), ())), preferred_element_type=F32)


def kernel(
    len_ref, slot_ref, samp_ref, samp_v, gain, qg, kg, freq,
    x_hbm, wq_hbm, km_hbm, vm_hbm, wo_hbm, kc_hbm, vc_hbm,
    own_ref, rem_ref,
    x_v, wq_v, km_v, vm_v, wo_v, kc_v, vc_v, vt_v, xs_v, nm_v, q_s,
    send_q, recv_q0, recv_q1, res_v, stat_v, last_v, send_r, recv_r, send_l, recv_l0, recv_l1,
    send_t, recv_t0, recv_t1, att_v, late_v, ofr_v, acc_v,
    sib_a, sib_b, part_a, part_b, part_c, own_v,
    x_sem, wq_sem, mat_sem, wo_sem, cache_sem,
    qs_sem, qr_sem, rs_sem, rr_sem, ls_sem, lr_sem, ss_sem, sr_sem, ts_sem, tr_sem, own_sem,
):
    recv_q, recv_l, recv_t = (recv_q0, recv_q1), (recv_l0, recv_l1), (recv_t0, recv_t1)
    me = lax.axis_index("group")
    rank = lax.axis_index("tensor")
    core = lax.rem(rank, 2)
    chip = rank // 2
    sibling = chip * 2 + (1 - core)
    remote = (1 - chip) * 2 + core
    far = (1 - chip) * 2 + (1 - core)

    x_copy = pltpu.make_async_copy(x_hbm, x_v, x_sem)
    x_copy.start()
    wq_copies = [
        pltpu.make_async_copy(
            wq_hbm.at[pl.ds(n * PIECE, PIECE), pl.ds(s * SEND_COLS, SEND_COLS)],
            wq_v.at[s, pl.ds(n * PIECE, PIECE)],
            wq_sem.at[s, n],
        )
        for s in range(SENDS)
        for n in range(PIECES)
    ]
    for copy in wq_copies[:DEPTH]:
        copy.start()
    mat_copies = [
        pltpu.make_async_copy(km_hbm, km_v, mat_sem.at[0]),
        pltpu.make_async_copy(vm_hbm, vm_v, mat_sem.at[1]),
    ]

    barrier = pltpu.get_barrier_semaphore()

    def greet(k, carry):
        pl.semaphore_signal(
            barrier, inc=1, device_id={"group": lax.rem(me + k, GROUPS)}, device_id_type=MESH
        )
        return carry

    lax.fori_loop(1, GROUPS, greet, 0)
    for other in (sibling, remote):
        pl.semaphore_signal(barrier, inc=1, device_id={"tensor": other}, device_id_type=MESH)

    lane = lax.broadcasted_iota(jnp.int32, (1, FLAT), 1)
    sub = lax.broadcasted_iota(jnp.int32, (ROWS, FLAT), 0)
    key_lane = jnp.zeros((1, FLAT), jnp.int32)
    key_sub = jnp.zeros((ROWS, FLAT), jnp.int32)
    len_lane = jnp.zeros((1, FLAT), F32)
    row_of_lane = lax.rem(lane, ROWS)
    owners = []
    for r in range(ROWS):
        prompt = samp_ref[me * ROWS + r]
        owner = lax.shift_right_logical(slot_ref[prompt], 1)
        owners.append(owner)
        order_key = owner * ROWS + r
        key_lane = jnp.where(row_of_lane == r, order_key, key_lane)
        key_sub = jnp.where(sub == r, order_key, key_sub)
        len_lane = jnp.where(row_of_lane == r, len_ref[prompt].astype(F32), len_lane)
    item_owner = []
    floor = jnp.int32(-1)
    for _ in range(ITEMS):
        best = jnp.int32(GROUPS)
        for owner in owners:
            best = jnp.where((owner > floor) & (owner < best), owner, best)
        item_owner.append(best)
        floor = best

    place = jnp.sum((key_sub < key_lane).astype(jnp.int32), axis=0, keepdims=True)
    q_id = lax.broadcasted_iota(jnp.int32, (FLAT, FLAT), 0)
    c_id = lax.broadcasted_iota(jnp.int32, (FLAT, FLAT), 1)
    step_q = lax.rem(q_id // 8, 2)
    chosen = (step_q == c_id // ROWS) & ((q_id // 16) * 8 + lax.rem(q_id, 8) == place)
    sorter = jnp.where(chosen, 1.0, 0.0).astype(BF16)
    step_sorter = jnp.where(q_id[:ROWS, :ROWS] == place[:, :ROWS], 1.0, 0.0).astype(BF16)
    position = jnp.sum(jnp.where(chosen, len_lane, 0.0), axis=1, keepdims=True)
    position = position + step_q[:, :1].astype(F32)
    angle = position * freq[...]
    cosine = jnp.cos(angle)
    half = lax.broadcasted_iota(jnp.int32, (FLAT, DIM), 1) < DIM // 2
    sine = jnp.sin(angle)
    sine = jnp.where(half, -sine, sine)

    def head(values, gains):
        mean = jnp.mean(values * values, axis=-1, keepdims=True)
        scaled = values * lax.rsqrt(mean + EPS) * gains
        return (scaled * cosine + pltpu.roll(scaled, DIM // 2, 1) * sine).astype(BF16)

    x_copy.wait()
    total = jnp.zeros((FLAT, 1), F32)
    for c in range(5):
        cols = slice(c * 1024, (c + 1) * 1024)
        part = jnp.dot(sorter, x_v[:, cols], preferred_element_type=F32)
        xs_v[:, cols] = part
        total = total + jnp.sum(part * part, axis=1, keepdims=True)
    scale = lax.rsqrt(total * (1.0 / WIDTH) + EPS)
    for c in range(5):
        cols = slice(c * 1024, (c + 1) * 1024)
        nm_v[:, cols] = (xs_v[:, cols] * scale * gain[:, cols]).astype(BF16)

    group_id = (
        lax.broadcasted_iota(jnp.int32, (8, 128), 0) * 4
        + lax.broadcasted_iota(jnp.int32, (8, 128), 1) // ROWS
    )
    limits, readers = [], []
    for p in range(2):
        prompt = jnp.int32(0)
        for i in range(64):
            prompt = jnp.where(slot_ref[i] == me * 2 + p, jnp.int32(i), prompt)
        limits.append(len_ref[prompt])
        hit = samp_v[...] == prompt
        readers.append(jnp.min(jnp.where(hit, group_id, GROUPS - 1)))
        readers.append(jnp.max(jnp.where(hit, group_id, 0)))


    def shuffled(n):
        return lax.rem(n * 7, GROUPS - 1) + 1

    def item_for(dest):
        found = jnp.int32(0)
        for i in range(ITEMS - 1):
            found = found + (dest > item_owner[i]).astype(jnp.int32)
        return found

    for s in range(SENDS):
        raw = None
        for n in range(PIECES):
            at = s * PIECES + n
            wq_copies[at].wait()
            if at + DEPTH < len(wq_copies):
                wq_copies[at + DEPTH].start()
            elif at + DEPTH == len(wq_copies):
                for copy in mat_copies:
                    copy.start()
            rows = slice(n * PIECE, (n + 1) * PIECE)
            part = jnp.dot(nm_v[:, rows], wq_v[s, rows], preferred_element_type=F32)
            raw = part if raw is None else raw + part
        for h in range(HALF_HEADS):
            turned = head(raw[:, h * DIM : (h + 1) * DIM], qg[...])
            at = (s * HALF_HEADS + h) * DIM
            q_s[:, :, at : at + DIM] = turned.reshape(ITEMS, 16, DIM)
        if s == 0:
            pl.semaphore_wait(barrier, GROUPS - 1 + 2)
        cols = slice(s * SEND_COLS, (s + 1) * SEND_COLS)
        recv_q[s][0] = q_s[item_for(me), :, cols]

        def send(n, carry):
            k = shuffled(n)
            dest = lax.rem(me + k, GROUPS)
            send_q[s, k] = q_s[item_for(dest), :, cols]
            pltpu.make_async_remote_copy(
                src_ref=send_q.at[s, k],
                dst_ref=recv_q[s].at[k],
                send_sem=qs_sem.at[s],
                recv_sem=qr_sem.at[s],
                device_id={"group": dest},
                device_id_type=MESH,
            ).start()
            return carry

        lax.fori_loop(0, GROUPS - 1, send, 0)

    cache_copies = [
        pltpu.make_async_copy(kc_hbm, kc_v, cache_sem.at[0]),
        pltpu.make_async_copy(vc_hbm, vc_v, cache_sem.at[1]),
    ]
    for copy in cache_copies:
        copy.start()
    wo_copies = []
    for b, block in enumerate((far, remote, sibling, rank)):
        copy = pltpu.make_async_copy(
            wo_hbm.at[:, pl.ds(pl.multiple_of(block * OUT_COLS, OUT_COLS), OUT_COLS)],
            wo_v.at[b],
            wo_sem.at[b],
        )
        copy.start()
        wo_copies.append(copy)

    for copy in mat_copies:
        copy.wait()
    fresh_key = head(jnp.dot(nm_v[...], km_v[...], preferred_element_type=F32), kg[...])
    fresh_value = jnp.dot(nm_v[...], vm_v[...], preferred_element_type=F32).astype(BF16)
    q_all = jnp.concatenate(
        [
            q_s[i, :, h * DIM : (h + 1) * DIM]
            for s in range(SENDS)
            for i in range(ITEMS)
            for h in range(s * HALF_HEADS, (s + 1) * HALF_HEADS)
        ],
        axis=0,
    )
    cells = (FLAT, ITEMS * DIM)
    row_id = lax.broadcasted_iota(jnp.int32, cells, 0)
    col_id = lax.broadcasted_iota(jnp.int32, cells, 1)
    seen = (
        (row_id // 16 == lax.rem(col_id // HALF_ROWS, ITEMS))
        & (lax.rem(row_id, 8) == lax.rem(col_id, 8))
        & (lax.rem(row_id // 8, 2) <= lax.rem(col_id // 8, 2))
    )
    fresh_score = jnp.where(seen, dot_nt(fresh_key, q_all) * SCALE, -1e30)
    fresh_peak = jnp.max(fresh_score, axis=0, keepdims=True)
    fresh_weight = jnp.where(seen, jnp.exp(fresh_score - fresh_peak), 0.0).astype(BF16)
    fresh_total = jnp.sum(fresh_weight.astype(F32), axis=0, keepdims=True)
    ofr_v[...] = dot_tn(fresh_weight, fresh_value)

    for copy in cache_copies:
        copy.wait()
    for p in range(2):
        vt_v[p] = vc_v[p].T

    key_id = lax.broadcasted_iota(jnp.int32, (SLOTS, DIM), 0)
    first_half = lax.broadcasted_iota(jnp.int32, (1, DIM), 1) < HALF_ROWS

    def result_for(dest):
        found = jnp.int32(0)
        for i in range(1, ITEMS):
            found = jnp.where(dest == readers[i], jnp.int32(i), found)
        return found

    for s in range(SENDS):
        pltpu.make_async_copy(
            send_q.at[s, pl.ds(1, GROUPS - 1)], recv_q[s].at[pl.ds(1, GROUPS - 1)], qr_sem.at[s]
        ).wait()
        for p in range(2):
            blocks = []
            for i in range(2):
                got = recv_q[s][lax.rem(me - readers[2 * p + i] + GROUPS, GROUPS)]
                blocks += [got[:, h * DIM : (h + 1) * DIM] for h in range(HALF_HEADS)]
            queries = jnp.concatenate(blocks, axis=0)
            valid = key_id < limits[p]
            score = jnp.where(valid, dot_nt(kc_v[p], queries) * SCALE, -1e30)
            peak = jnp.max(score, axis=0, keepdims=True)
            weight = jnp.where(valid, jnp.exp(score - peak), 0.0).astype(BF16)
            amount = jnp.sum(weight.astype(F32), axis=0, keepdims=True)
            summed = jnp.dot(vt_v[p], weight, preferred_element_type=F32).T
            for i in range(2):
                own = summed[i * HALF_ROWS : (i + 1) * HALF_ROWS]
                if s == 0:
                    res_v[2 * p + i] = own.astype(BF16)
                    continue
                for t in range(2):
                    rows = [own[h * 16 + t * 8 : h * 16 + t * 8 + 8] for h in range(HALF_HEADS)]
                    last_v[t, 2 * p + i] = jnp.concatenate(rows, axis=0).astype(BF16)
            peak_turned = pltpu.roll(peak, HALF_ROWS, 1)
            amount_turned = pltpu.roll(amount, HALF_ROWS, 1)
            stat_v[s, 2 * p] = jnp.where(first_half, peak, amount_turned)
            stat_v[s, 2 * p + 1] = jnp.where(first_half, peak_turned, amount)

        if s == 0:
            trips = [(res_v, send_r, recv_r, rs_sem, rr_sem)]
        else:
            trips = [
                (last_v.at[t], send_l.at[t], recv_l[t], ls_sem.at[t], lr_sem.at[t])
                for t in range(2)
            ]
        trips = [(stat_v.at[s], send_t.at[s], recv_t[s], ss_sem.at[s], sr_sem.at[s])] + trips
        for source, sent, got_back, send_sem, recv_sem in trips:
            got_back[0] = source[result_for(me)]

            def give_back(n, carry):
                k = shuffled(n)
                dest = lax.rem(me + k, GROUPS)
                sent[k] = source[result_for(dest)]
                pltpu.make_async_remote_copy(
                    src_ref=sent.at[k],
                    dst_ref=got_back.at[k],
                    send_sem=send_sem,
                    recv_sem=recv_sem,
                    device_id={"group": dest},
                    device_id_type=MESH,
                ).start()
                return carry

            lax.fori_loop(0, GROUPS - 1, give_back, 0)

    def wait_all(sent, got_back, sem):
        others = pl.ds(1, GROUPS - 1)
        pltpu.make_async_copy(sent.at[others], got_back.at[others], sem).wait()

    places = [lax.rem(me - owner + GROUPS, GROUPS) for owner in item_owner]
    factor_id = lax.broadcasted_iota(jnp.int32, (8, ITEMS * HALF_ROWS), 0)

    def factors_of(s):
        wait_all(send_t.at[s], recv_t[s], sr_sem.at[s])
        stats = [recv_t[s][at] for at in places]
        peak = jnp.concatenate([stat[:, :HALF_ROWS] for stat in stats], axis=1)
        amount = jnp.concatenate([stat[:, HALF_ROWS:] for stat in stats], axis=1)
        cols = slice(s * ITEMS * HALF_ROWS, (s + 1) * ITEMS * HALF_ROWS)
        own_peak = fresh_peak[:, cols]
        joint = jnp.maximum(peak, own_peak)
        early = jnp.exp(peak - joint)
        late = jnp.exp(own_peak - joint)
        lower = amount * early + fresh_total[:, cols] * late
        return jnp.where(factor_id == 0, early / lower, late / lower).T

    factors = factors_of(0)
    wait_all(send_r, recv_r, rr_sem)
    for i in range(ITEMS):
        rows = slice(i * HALF_ROWS, (i + 1) * HALF_ROWS)
        done = recv_r[places[i]].astype(F32) * factors[rows, 0:1] + ofr_v[rows] * factors[rows, 1:2]
        done = done.astype(BF16)
        for h in range(HALF_HEADS):
            att_v[i * 16 : (i + 1) * 16, h * DIM : (h + 1) * DIM] = done[h * 16 : (h + 1) * 16]
    attended = dot_tn(sorter, att_v[...]).astype(BF16)
    for block in range(TENSOR):
        wo_copies[block].wait()
        acc_v[block] = jnp.dot(
            attended, wo_v[block, : HALF_HEADS * DIM], preferred_element_type=F32
        )
    factors = factors_of(1)

    def merge_step(t):
        wait_all(send_l.at[t], recv_l[t], lr_sem.at[t])
        for i in range(ITEMS):
            got = recv_l[t][places[i]].astype(F32)
            for h in range(HALF_HEADS):
                at = i * HALF_ROWS + h * 16 + t * 8
                done = got[h * 8 : (h + 1) * 8] * factors[at : at + 8, 0:1]
                fresh = ofr_v[ITEMS * HALF_ROWS + at : ITEMS * HALF_ROWS + at + 8]
                late_v[t, i * 8 : (i + 1) * 8, h * DIM : (h + 1) * DIM] = (
                    done + fresh * factors[at : at + 8, 1:2]
                )
        return dot_tn(step_sorter, late_v[t].astype(BF16)).astype(BF16)

    def pass_on(n, source, target, device):
        return pltpu.make_async_remote_copy(
            src_ref=source,
            dst_ref=target,
            send_sem=ts_sem.at[n],
            recv_sem=tr_sem.at[n],
            device_id={"tensor": device},
            device_id_type=MESH,
        )

    first, second, third, own_copies = [], [], [], []
    for t in range(2):
        attended = merge_step(t)

        def project(block):
            last = jnp.dot(
                attended, wo_v[block, HALF_HEADS * DIM :], preferred_element_type=F32
            )
            return acc_v[block, t * ROWS : (t + 1) * ROWS] + last

        part_a[t] = project(0).astype(BF16)
        first.append(pass_on(t, part_a.at[t], sib_a.at[t], sibling))
        first[t].start()
        mine = project(1)
        part_c[t] = project(2).astype(BF16)
        third.append(pass_on(4 + t, part_c.at[t], sib_b.at[t], sibling))
        third[t].start()
        first[t].wait_recv()
        part_b[t] = (mine + sib_a[t].astype(F32)).astype(BF16)
        second.append(pass_on(2 + t, part_b.at[t], rem_ref.at[t], remote))
        second[t].start()
        mine = project(3)
        third[t].wait_recv()
        own_v[t] = mine + sib_b[t].astype(F32)
        own_copies.append(pltpu.make_async_copy(own_v.at[t], own_ref.at[t], own_sem.at[t]))
        own_copies[t].start()
    for t in range(2):
        second[t].wait_recv()
        own_copies[t].wait()

    for copy in first + second + third:
        copy.wait_send()
    for s in range(SENDS):
        pltpu.make_async_copy(
            send_q.at[s, pl.ds(1, GROUPS - 1)], recv_q[s].at[pl.ds(1, GROUPS - 1)], qs_sem.at[s]
        ).wait()
    wait_all(send_r, recv_r, rs_sem)
    for s in range(2):
        wait_all(send_t.at[s], recv_t[s], ss_sem.at[s])
        wait_all(send_l.at[s], recv_l[s], ls_sem.at[s])


def shards(
    inputs,
    attn_gain,
    w_query,
    key_matrix,
    value_matrix,
    q_gain,
    k_gain,
    w_out,
    prompt_key_cache,
    prompt_value_cache,
    prompt_lengths,
    prompt_slot,
    sample_prompt,
):
    half = np.arange(DIM // 2, dtype=np.float64)
    frequency = ROPE_BASE ** (-(half * 2.0 / DIM))
    frequency = jnp.asarray(np.concatenate([frequency, frequency])[None, :], F32)
    smem = pl.BlockSpec(memory_space=pltpu.SMEM)
    vmem = pl.BlockSpec(memory_space=pltpu.VMEM)
    anywhere = pl.BlockSpec(memory_space=pl.ANY)
    dma = pltpu.SemaphoreType.DMA
    own, other = pl.pallas_call(
        kernel,
        out_shape=(
            jax.ShapeDtypeStruct((2, ROWS, OUT_COLS), F32),
            jax.ShapeDtypeStruct((2, ROWS, OUT_COLS), BF16),
        ),
        in_specs=[smem] * 3 + [vmem] * 5 + [anywhere] * 7,
        out_specs=(anywhere, anywhere),
        scratch_shapes=[
            pltpu.VMEM((FLAT, WIDTH), BF16),
            pltpu.VMEM((SENDS, WIDTH, SEND_COLS), BF16),
            pltpu.VMEM((WIDTH, DIM), BF16),
            pltpu.VMEM((WIDTH, DIM), BF16),
            pltpu.VMEM((TENSOR, QCOLS, OUT_COLS), BF16),
            pltpu.VMEM((2, SLOTS, DIM), BF16),
            pltpu.VMEM((2, SLOTS, DIM), BF16),
            pltpu.VMEM((2, DIM, SLOTS), BF16),
            pltpu.VMEM((FLAT, WIDTH), F32),
            pltpu.VMEM((FLAT, WIDTH), BF16),
            pltpu.VMEM((ITEMS, 16, QCOLS), BF16),
            pltpu.VMEM((SENDS, GROUPS, 16, SEND_COLS), BF16),
            pltpu.VMEM((GROUPS, 16, SEND_COLS), BF16),
            pltpu.VMEM((GROUPS, 16, SEND_COLS), BF16),
            pltpu.VMEM((ITEMS, HALF_ROWS, DIM), BF16),
            pltpu.VMEM((SENDS, ITEMS, 1, DIM), F32),
            pltpu.VMEM((2, ITEMS, STEP_ROWS, DIM), BF16),
            pltpu.VMEM((GROUPS, HALF_ROWS, DIM), BF16),
            pltpu.VMEM((GROUPS, HALF_ROWS, DIM), BF16),
            pltpu.VMEM((2, GROUPS, STEP_ROWS, DIM), BF16),
            pltpu.VMEM((GROUPS, STEP_ROWS, DIM), BF16),
            pltpu.VMEM((GROUPS, STEP_ROWS, DIM), BF16),
            pltpu.VMEM((SENDS, GROUPS, 1, DIM), F32),
            pltpu.VMEM((GROUPS, 1, DIM), F32),
            pltpu.VMEM((GROUPS, 1, DIM), F32),
            pltpu.VMEM((FLAT, SEND_COLS), BF16),
            pltpu.VMEM((2, ROWS, SEND_COLS), F32),
            pltpu.VMEM((ITEMS * DIM, DIM), F32),
            pltpu.VMEM((TENSOR, FLAT, OUT_COLS), F32),
            pltpu.VMEM((2, ROWS, OUT_COLS), BF16),
            pltpu.VMEM((2, ROWS, OUT_COLS), BF16),
            pltpu.VMEM((2, ROWS, OUT_COLS), BF16),
            pltpu.VMEM((2, ROWS, OUT_COLS), BF16),
            pltpu.VMEM((2, ROWS, OUT_COLS), BF16),
            pltpu.VMEM((2, ROWS, OUT_COLS), F32),
            dma,
            dma((SENDS, PIECES)),
            dma((2,)),
            dma((TENSOR,)),
            dma((2,)),
            dma((SENDS,)),
            dma((SENDS,)),
            dma,
            dma,
            dma((2,)),
            dma((2,)),
            dma((SENDS,)),
            dma((SENDS,)),
            dma((6,)),
            dma((6,)),
            dma((2,)),
        ],
        compiler_params=pltpu.CompilerParams(
            collective_id=0, has_side_effects=True, vmem_limit_bytes=56 * 1024 * 1024
        ),
    )(
        prompt_lengths,
        prompt_slot,
        sample_prompt,
        sample_prompt.reshape(8, 128),
        attn_gain.reshape(1, WIDTH),
        q_gain.reshape(1, DIM),
        k_gain.reshape(1, DIM),
        frequency,
        inputs.reshape(FLAT, WIDTH),
        w_query,
        key_matrix,
        value_matrix,
        w_out,
        prompt_key_cache,
        prompt_value_cache,
    )
    return (own + other.astype(F32)).astype(BF16)


def solution(mesh):
    in_specs = (
        P(None, "group", None),
        P(),
        P(None, "tensor"),
        P(None, "tensor"),
        P(None, "tensor"),
        P(),
        P(),
        P("tensor", None),
        P("group", None, "tensor"),
        P("group", None, "tensor"),
        P(),
        P(),
        P(),
    )
    out_specs = P(None, "group", "tensor")
    return jax.shard_map(shards, mesh=mesh, in_specs=in_specs, out_specs=out_specs, check_vma=False)
```

```python
import jax
import jax.numpy as jnp
import numpy as np
from jax import lax
from jax.experimental import pallas as pl
from jax.experimental.pallas import tpu as pltpu
from jax.sharding import PartitionSpec as P

MESH = pl.DeviceIdType.MESH
EPS = 1e-06
ROPE_BASE = 1000000.0
GROUPS = 32
TENSOR = 4
ROWS = 32
ITEMS = 4
HEADS = 8
DIM = 128
WIDTH = 5120
QCOLS = HEADS * DIM
SLOTS = 1024
FLAT = 2 * ROWS
DEPTH = 2
SENDS = 2
SEND_COLS = QCOLS // SENDS
OUT_COLS = WIDTH // TENSOR
HALF_HEADS = HEADS // SENDS
HALF_ROWS = HALF_HEADS * 16
PIECES = 2
PIECE = WIDTH // PIECES
STEP_ROWS = HALF_HEADS * 8
SCALE = 1.0 / (DIM**0.5)
F32 = jnp.float32
BF16 = jnp.bfloat16


def dot_nt(a, b):
    return lax.dot_general(a, b, (((1,), (1,)), ((), ())), preferred_element_type=F32)


def dot_tn(a, b):
    return lax.dot_general(a, b, (((0,), (0,)), ((), ())), preferred_element_type=F32)


def kernel(
    len_ref, slot_ref, samp_ref, samp_v, gain, qg, kg, freq,
    x_hbm, wq_hbm, km_hbm, vm_hbm, wo_hbm, kc_hbm, vc_hbm,
    own_ref, rem_ref,
    x_v, wq_v, km_v, vm_v, wo_v, kc_v, vc_v, vt_v, xs_v, nm_v, q_s,
    send_q, recv_q0, recv_q1, res_v, stat_v, last_v, send_r, recv_r, send_l, recv_l0, recv_l1,
    send_t, recv_t0, recv_t1, att_v, late_v, ofr_v, acc_v,
    sib_a, sib_b, part_a, part_b, part_c,
    x_sem, wq_sem, mat_sem, wo_sem, cache_sem,
    qs_sem, qr_sem, rs_sem, rr_sem, ls_sem, lr_sem, ss_sem, sr_sem, ts_sem, tr_sem,
):
    recv_q, recv_l, recv_t = (recv_q0, recv_q1), (recv_l0, recv_l1), (recv_t0, recv_t1)
    me = lax.axis_index("group")
    rank = lax.axis_index("tensor")
    core = lax.rem(rank, 2)
    chip = rank // 2
    sibling = chip * 2 + (1 - core)
    remote = (1 - chip) * 2 + core
    far = (1 - chip) * 2 + (1 - core)

    x_copy = pltpu.make_async_copy(x_hbm, x_v, x_sem)
    x_copy.start()
    wq_copies = [
        pltpu.make_async_copy(
            wq_hbm.at[pl.ds(n * PIECE, PIECE), pl.ds(s * SEND_COLS, SEND_COLS)],
            wq_v.at[s, pl.ds(n * PIECE, PIECE)],
            wq_sem.at[s, n],
        )
        for s in range(SENDS)
        for n in range(PIECES)
    ]
    for copy in wq_copies[:DEPTH]:
        copy.start()
    mat_copies = [
        pltpu.make_async_copy(km_hbm, km_v, mat_sem.at[0]),
        pltpu.make_async_copy(vm_hbm, vm_v, mat_sem.at[1]),
    ]

    barrier = pltpu.get_barrier_semaphore()

    def greet(k, carry):
        pl.semaphore_signal(
            barrier, inc=1, device_id={"group": lax.rem(me + k, GROUPS)}, device_id_type=MESH
        )
        return carry

    lax.fori_loop(1, GROUPS, greet, 0)
    for other in (sibling, remote):
        pl.semaphore_signal(barrier, inc=1, device_id={"tensor": other}, device_id_type=MESH)

    lane = lax.broadcasted_iota(jnp.int32, (1, FLAT), 1)
    sub = lax.broadcasted_iota(jnp.int32, (ROWS, FLAT), 0)
    key_lane = jnp.zeros((1, FLAT), jnp.int32)
    key_sub = jnp.zeros((ROWS, FLAT), jnp.int32)
    len_lane = jnp.zeros((1, FLAT), F32)
    row_of_lane = lax.rem(lane, ROWS)
    owners = []
    for r in range(ROWS):
        prompt = samp_ref[me * ROWS + r]
        owner = lax.shift_right_logical(slot_ref[prompt], 1)
        owners.append(owner)
        order_key = owner * ROWS + r
        key_lane = jnp.where(row_of_lane == r, order_key, key_lane)
        key_sub = jnp.where(sub == r, order_key, key_sub)
        len_lane = jnp.where(row_of_lane == r, len_ref[prompt].astype(F32), len_lane)
    place = jnp.sum((key_sub < key_lane).astype(jnp.int32), axis=0, keepdims=True)
    q_id = lax.broadcasted_iota(jnp.int32, (FLAT, FLAT), 0)
    c_id = lax.broadcasted_iota(jnp.int32, (FLAT, FLAT), 1)
    step_q = lax.rem(q_id // 8, 2)
    chosen = (step_q == c_id // ROWS) & ((q_id // 16) * 8 + lax.rem(q_id, 8) == place)
    sorter = jnp.where(chosen, 1.0, 0.0).astype(BF16)
    step_sorter = jnp.where(q_id[:ROWS, :ROWS] == place[:, :ROWS], 1.0, 0.0).astype(BF16)
    position = jnp.sum(jnp.where(chosen, len_lane, 0.0), axis=1, keepdims=True)
    position = position + step_q[:, :1].astype(F32)
    angle = position * freq[...]
    cosine = jnp.cos(angle)
    half = lax.broadcasted_iota(jnp.int32, (FLAT, DIM), 1) < DIM // 2
    sine = jnp.sin(angle)
    sine = jnp.where(half, -sine, sine)

    def head(values, gains):
        mean = jnp.mean(values * values, axis=-1, keepdims=True)
        scaled = values * lax.rsqrt(mean + EPS) * gains
        return (scaled * cosine + pltpu.roll(scaled, DIM // 2, 1) * sine).astype(BF16)

    x_copy.wait()
    total = jnp.zeros((FLAT, 1), F32)
    for c in range(5):
        cols = slice(c * 1024, (c + 1) * 1024)
        part = jnp.dot(sorter, x_v[:, cols], preferred_element_type=F32)
        xs_v[:, cols] = part
        total = total + jnp.sum(part * part, axis=1, keepdims=True)
    item_owner = []
    floor = jnp.int32(-1)
    for _ in range(ITEMS):
        best = jnp.int32(GROUPS)
        for owner in owners:
            best = jnp.where((owner > floor) & (owner < best), owner, best)
        item_owner.append(best)
        floor = best

    scale = lax.rsqrt(total * (1.0 / WIDTH) + EPS)
    for c in range(5):
        cols = slice(c * 1024, (c + 1) * 1024)
        nm_v[:, cols] = (xs_v[:, cols] * scale * gain[:, cols]).astype(BF16)

    def shuffled(n):
        return lax.rem(n * 7, GROUPS - 1) + 1

    def item_for(dest):
        found = jnp.int32(0)
        for i in range(ITEMS - 1):
            found = found + (dest > item_owner[i]).astype(jnp.int32)
        return found

    for s in range(SENDS):
        raw = None
        for n in range(PIECES):
            at = s * PIECES + n
            wq_copies[at].wait()
            if at + DEPTH < len(wq_copies):
                wq_copies[at + DEPTH].start()
            elif at + DEPTH == len(wq_copies):
                for copy in mat_copies:
                    copy.start()
            rows = slice(n * PIECE, (n + 1) * PIECE)
            part = jnp.dot(nm_v[:, rows], wq_v[s, rows], preferred_element_type=F32)
            raw = part if raw is None else raw + part
        for h in range(HALF_HEADS):
            turned = head(raw[:, h * DIM : (h + 1) * DIM], qg[...])
            at = (s * HALF_HEADS + h) * DIM
            q_s[:, :, at : at + DIM] = turned.reshape(ITEMS, 16, DIM)
        if s == 0:
            pl.semaphore_wait(barrier, GROUPS - 1 + 2)
        cols = slice(s * SEND_COLS, (s + 1) * SEND_COLS)
        recv_q[s][0] = q_s[item_for(me), :, cols]

        def send(n, carry):
            k = shuffled(n)
            dest = lax.rem(me + k, GROUPS)
            send_q[s, k] = q_s[item_for(dest), :, cols]
            pltpu.make_async_remote_copy(
                src_ref=send_q.at[s, k],
                dst_ref=recv_q[s].at[k],
                send_sem=qs_sem.at[s],
                recv_sem=qr_sem.at[s],
                device_id={"group": dest},
                device_id_type=MESH,
            ).start()
            return carry

        lax.fori_loop(0, GROUPS - 1, send, 0)

    cache_copies = [
        pltpu.make_async_copy(kc_hbm, kc_v, cache_sem.at[0]),
        pltpu.make_async_copy(vc_hbm, vc_v, cache_sem.at[1]),
    ]
    for copy in cache_copies:
        copy.start()
    wo_copies = []
    for b, block in enumerate((far, remote, sibling, rank)):
        copy = pltpu.make_async_copy(
            wo_hbm.at[:, pl.ds(pl.multiple_of(block * OUT_COLS, OUT_COLS), OUT_COLS)],
            wo_v.at[b],
            wo_sem.at[b],
        )
        copy.start()
        wo_copies.append(copy)

    group_id = (
        lax.broadcasted_iota(jnp.int32, (8, 128), 0) * 4
        + lax.broadcasted_iota(jnp.int32, (8, 128), 1) // ROWS
    )
    limits, readers = [], []
    for p in range(2):
        prompt = jnp.int32(0)
        for i in range(64):
            prompt = jnp.where(slot_ref[i] == me * 2 + p, jnp.int32(i), prompt)
        limits.append(len_ref[prompt])
        hit = samp_v[...] == prompt
        readers.append(jnp.min(jnp.where(hit, group_id, GROUPS - 1)))
        readers.append(jnp.max(jnp.where(hit, group_id, 0)))


    for copy in mat_copies:
        copy.wait()
    fresh_key = head(jnp.dot(nm_v[...], km_v[...], preferred_element_type=F32), kg[...])
    fresh_value = jnp.dot(nm_v[...], vm_v[...], preferred_element_type=F32).astype(BF16)
    q_all = jnp.concatenate(
        [
            q_s[i, :, h * DIM : (h + 1) * DIM]
            for s in range(SENDS)
            for i in range(ITEMS)
            for h in range(s * HALF_HEADS, (s + 1) * HALF_HEADS)
        ],
        axis=0,
    )
    cells = (FLAT, ITEMS * DIM)
    row_id = lax.broadcasted_iota(jnp.int32, cells, 0)
    col_id = lax.broadcasted_iota(jnp.int32, cells, 1)
    seen = (
        (row_id // 16 == lax.rem(col_id // HALF_ROWS, ITEMS))
        & (lax.rem(row_id, 8) == lax.rem(col_id, 8))
        & (lax.rem(row_id // 8, 2) <= lax.rem(col_id // 8, 2))
    )
    fresh_score = jnp.where(seen, dot_nt(fresh_key, q_all) * SCALE, -1e30)
    fresh_peak = jnp.max(fresh_score, axis=0, keepdims=True)
    fresh_weight = jnp.where(seen, jnp.exp(fresh_score - fresh_peak), 0.0).astype(BF16)
    fresh_total = jnp.sum(fresh_weight.astype(F32), axis=0, keepdims=True)
    ofr_v[...] = dot_tn(fresh_weight, fresh_value)

    for copy in cache_copies:
        copy.wait()
    for p in range(2):
        vt_v[p] = vc_v[p].T

    key_id = lax.broadcasted_iota(jnp.int32, (SLOTS, DIM), 0)
    first_half = lax.broadcasted_iota(jnp.int32, (1, DIM), 1) < HALF_ROWS

    def result_for(dest):
        found = jnp.int32(0)
        for i in range(1, ITEMS):
            found = jnp.where(dest == readers[i], jnp.int32(i), found)
        return found

    for s in range(SENDS):
        pltpu.make_async_copy(
            send_q.at[s, pl.ds(1, GROUPS - 1)], recv_q[s].at[pl.ds(1, GROUPS - 1)], qr_sem.at[s]
        ).wait()
        for p in range(2):
            blocks = []
            for i in range(2):
                got = recv_q[s][lax.rem(me - readers[2 * p + i] + GROUPS, GROUPS)]
                blocks += [got[:, h * DIM : (h + 1) * DIM] for h in range(HALF_HEADS)]
            queries = jnp.concatenate(blocks, axis=0)
            valid = key_id < limits[p]
            score = jnp.where(valid, dot_nt(kc_v[p], queries) * SCALE, -1e30)
            peak = jnp.max(score, axis=0, keepdims=True)
            weight = jnp.where(valid, jnp.exp(score - peak), 0.0).astype(BF16)
            amount = jnp.sum(weight.astype(F32), axis=0, keepdims=True)
            summed = jnp.dot(vt_v[p], weight, preferred_element_type=F32).T
            for i in range(2):
                own = summed[i * HALF_ROWS : (i + 1) * HALF_ROWS]
                if s == 0:
                    res_v[2 * p + i] = own.astype(BF16)
                    continue
                for t in range(2):
                    rows = [own[h * 16 + t * 8 : h * 16 + t * 8 + 8] for h in range(HALF_HEADS)]
                    last_v[t, 2 * p + i] = jnp.concatenate(rows, axis=0).astype(BF16)
            peak_turned = pltpu.roll(peak, HALF_ROWS, 1)
            amount_turned = pltpu.roll(amount, HALF_ROWS, 1)
            stat_v[s, 2 * p] = jnp.where(first_half, peak, amount_turned)
            stat_v[s, 2 * p + 1] = jnp.where(first_half, peak_turned, amount)

        if s == 0:
            trips = [(res_v, send_r, recv_r, rs_sem, rr_sem)]
        else:
            trips = [
                (last_v.at[t], send_l.at[t], recv_l[t], ls_sem.at[t], lr_sem.at[t])
                for t in range(2)
            ]
        trips = [(stat_v.at[s], send_t.at[s], recv_t[s], ss_sem.at[s], sr_sem.at[s])] + trips
        for source, sent, got_back, send_sem, recv_sem in trips:
            got_back[0] = source[result_for(me)]

            def give_back(n, carry):
                k = shuffled(n)
                dest = lax.rem(me + k, GROUPS)
                sent[k] = source[result_for(dest)]
                pltpu.make_async_remote_copy(
                    src_ref=sent.at[k],
                    dst_ref=got_back.at[k],
                    send_sem=send_sem,
                    recv_sem=recv_sem,
                    device_id={"group": dest},
                    device_id_type=MESH,
                ).start()
                return carry

            lax.fori_loop(0, GROUPS - 1, give_back, 0)

    def wait_all(sent, got_back, sem):
        others = pl.ds(1, GROUPS - 1)
        pltpu.make_async_copy(sent.at[others], got_back.at[others], sem).wait()

    places = [lax.rem(me - owner + GROUPS, GROUPS) for owner in item_owner]
    factor_id = lax.broadcasted_iota(jnp.int32, (8, ITEMS * HALF_ROWS), 0)

    def factors_of(s):
        wait_all(send_t.at[s], recv_t[s], sr_sem.at[s])
        stats = [recv_t[s][at] for at in places]
        peak = jnp.concatenate([stat[:, :HALF_ROWS] for stat in stats], axis=1)
        amount = jnp.concatenate([stat[:, HALF_ROWS:] for stat in stats], axis=1)
        cols = slice(s * ITEMS * HALF_ROWS, (s + 1) * ITEMS * HALF_ROWS)
        own_peak = fresh_peak[:, cols]
        joint = jnp.maximum(peak, own_peak)
        early = jnp.exp(peak - joint)
        late = jnp.exp(own_peak - joint)
        lower = amount * early + fresh_total[:, cols] * late
        return jnp.where(factor_id == 0, early / lower, late / lower).T

    factors = factors_of(0)
    wait_all(send_r, recv_r, rr_sem)
    for i in range(ITEMS):
        rows = slice(i * HALF_ROWS, (i + 1) * HALF_ROWS)
        done = recv_r[places[i]].astype(F32) * factors[rows, 0:1] + ofr_v[rows] * factors[rows, 1:2]
        done = done.astype(BF16)
        for h in range(HALF_HEADS):
            att_v[i * 16 : (i + 1) * 16, h * DIM : (h + 1) * DIM] = done[h * 16 : (h + 1) * 16]
    attended = dot_tn(sorter, att_v[...]).astype(BF16)
    for block in range(TENSOR):
        wo_copies[block].wait()
        acc_v[block] = jnp.dot(
            attended, wo_v[block, : HALF_HEADS * DIM], preferred_element_type=F32
        )
    factors = factors_of(1)

    def merge_step(t):
        wait_all(send_l.at[t], recv_l[t], lr_sem.at[t])
        for i in range(ITEMS):
            got = recv_l[t][places[i]].astype(F32)
            for h in range(HALF_HEADS):
                at = i * HALF_ROWS + h * 16 + t * 8
                done = got[h * 8 : (h + 1) * 8] * factors[at : at + 8, 0:1]
                fresh = ofr_v[ITEMS * HALF_ROWS + at : ITEMS * HALF_ROWS + at + 8]
                late_v[t, i * 8 : (i + 1) * 8, h * DIM : (h + 1) * DIM] = (
                    done + fresh * factors[at : at + 8, 1:2]
                )
        return dot_tn(step_sorter, late_v[t].astype(BF16)).astype(BF16)

    def pass_on(n, source, target, device):
        return pltpu.make_async_remote_copy(
            src_ref=source,
            dst_ref=target,
            send_sem=ts_sem.at[n],
            recv_sem=tr_sem.at[n],
            device_id={"tensor": device},
            device_id_type=MESH,
        )

    first, second, third = [], [], []
    for t in range(2):
        attended = merge_step(t)

        def project(block):
            last = jnp.dot(
                attended, wo_v[block, HALF_HEADS * DIM :], preferred_element_type=F32
            )
            return acc_v[block, t * ROWS : (t + 1) * ROWS] + last

        part_a[t] = project(0).astype(BF16)
        first.append(pass_on(t, part_a.at[t], sib_a.at[t], sibling))
        first[t].start()
        mine = project(1)
        part_c[t] = project(2).astype(BF16)
        third.append(pass_on(4 + t, part_c.at[t], sib_b.at[t], sibling))
        third[t].start()
        first[t].wait_recv()
        part_b[t] = (mine + sib_a[t].astype(F32)).astype(BF16)
        second.append(pass_on(2 + t, part_b.at[t], rem_ref.at[t], remote))
        second[t].start()
        mine = project(3)
        third[t].wait_recv()
        own_ref[t] = mine + sib_b[t].astype(F32)
    for t in range(2):
        second[t].wait_recv()

    for copy in first + second + third:
        copy.wait_send()
    for s in range(SENDS):
        pltpu.make_async_copy(
            send_q.at[s, pl.ds(1, GROUPS - 1)], recv_q[s].at[pl.ds(1, GROUPS - 1)], qs_sem.at[s]
        ).wait()
    wait_all(send_r, recv_r, rs_sem)
    for s in range(2):
        wait_all(send_t.at[s], recv_t[s], ss_sem.at[s])
        wait_all(send_l.at[s], recv_l[s], ls_sem.at[s])


def shards(
    inputs,
    attn_gain,
    w_query,
    key_matrix,
    value_matrix,
    q_gain,
    k_gain,
    w_out,
    prompt_key_cache,
    prompt_value_cache,
    prompt_lengths,
    prompt_slot,
    sample_prompt,
):
    half = np.arange(DIM // 2, dtype=np.float64)
    frequency = ROPE_BASE ** (-(half * 2.0 / DIM))
    frequency = jnp.asarray(np.concatenate([frequency, frequency])[None, :], F32)
    smem = pl.BlockSpec(memory_space=pltpu.SMEM)
    vmem = pl.BlockSpec(memory_space=pltpu.VMEM)
    anywhere = pl.BlockSpec(memory_space=pl.ANY)
    dma = pltpu.SemaphoreType.DMA
    own, other = pl.pallas_call(
        kernel,
        out_shape=(
            pltpu.VMEM((2, ROWS, OUT_COLS), F32),
            pltpu.VMEM((2, ROWS, OUT_COLS), BF16),
        ),
        in_specs=[smem] * 3 + [vmem] * 5 + [anywhere] * 7,
        out_specs=(vmem, vmem),
        scratch_shapes=[
            pltpu.VMEM((FLAT, WIDTH), BF16),
            pltpu.VMEM((SENDS, WIDTH, SEND_COLS), BF16),
            pltpu.VMEM((WIDTH, DIM), BF16),
            pltpu.VMEM((WIDTH, DIM), BF16),
            pltpu.VMEM((TENSOR, QCOLS, OUT_COLS), BF16),
            pltpu.VMEM((2, SLOTS, DIM), BF16),
            pltpu.VMEM((2, SLOTS, DIM), BF16),
            pltpu.VMEM((2, DIM, SLOTS), BF16),
            pltpu.VMEM((FLAT, WIDTH), F32),
            pltpu.VMEM((FLAT, WIDTH), BF16),
            pltpu.VMEM((ITEMS, 16, QCOLS), BF16),
            pltpu.VMEM((SENDS, GROUPS, 16, SEND_COLS), BF16),
            pltpu.VMEM((GROUPS, 16, SEND_COLS), BF16),
            pltpu.VMEM((GROUPS, 16, SEND_COLS), BF16),
            pltpu.VMEM((ITEMS, HALF_ROWS, DIM), BF16),
            pltpu.VMEM((SENDS, ITEMS, 1, DIM), F32),
            pltpu.VMEM((2, ITEMS, STEP_ROWS, DIM), BF16),
            pltpu.VMEM((GROUPS, HALF_ROWS, DIM), BF16),
            pltpu.VMEM((GROUPS, HALF_ROWS, DIM), BF16),
            pltpu.VMEM((2, GROUPS, STEP_ROWS, DIM), BF16),
            pltpu.VMEM((GROUPS, STEP_ROWS, DIM), BF16),
            pltpu.VMEM((GROUPS, STEP_ROWS, DIM), BF16),
            pltpu.VMEM((SENDS, GROUPS, 1, DIM), F32),
            pltpu.VMEM((GROUPS, 1, DIM), F32),
            pltpu.VMEM((GROUPS, 1, DIM), F32),
            pltpu.VMEM((FLAT, SEND_COLS), BF16),
            pltpu.VMEM((2, ROWS, SEND_COLS), F32),
            pltpu.VMEM((ITEMS * DIM, DIM), F32),
            pltpu.VMEM((TENSOR, FLAT, OUT_COLS), F32),
            pltpu.VMEM((2, ROWS, OUT_COLS), BF16),
            pltpu.VMEM((2, ROWS, OUT_COLS), BF16),
            pltpu.VMEM((2, ROWS, OUT_COLS), BF16),
            pltpu.VMEM((2, ROWS, OUT_COLS), BF16),
            pltpu.VMEM((2, ROWS, OUT_COLS), BF16),
            dma,
            dma((SENDS, PIECES)),
            dma((2,)),
            dma((TENSOR,)),
            dma((2,)),
            dma((SENDS,)),
            dma((SENDS,)),
            dma,
            dma,
            dma((2,)),
            dma((2,)),
            dma((SENDS,)),
            dma((SENDS,)),
            dma((6,)),
            dma((6,)),
        ],
        compiler_params=pltpu.CompilerParams(
            collective_id=0, has_side_effects=True, vmem_limit_bytes=56 * 1024 * 1024
        ),
    )(
        prompt_lengths,
        prompt_slot,
        sample_prompt,
        sample_prompt.reshape(8, 128),
        attn_gain.reshape(1, WIDTH),
        q_gain.reshape(1, DIM),
        k_gain.reshape(1, DIM),
        frequency,
        inputs.reshape(FLAT, WIDTH),
        w_query,
        key_matrix,
        value_matrix,
        w_out,
        prompt_key_cache,
        prompt_value_cache,
    )
    return (own + other.astype(F32)).astype(BF16)


def solution(mesh):
    in_specs = (
        P(None, "group", None),
        P(),
        P(None, "tensor"),
        P(None, "tensor"),
        P(None, "tensor"),
        P(),
        P(),
        P("tensor", None),
        P("group", None, "tensor"),
        P("group", None, "tensor"),
        P(),
        P(),
        P(),
    )
    out_specs = P(None, "group", "tensor")
    return jax.shard_map(shards, mesh=mesh, in_specs=in_specs, out_specs=out_specs, check_vma=False)
```

```python
import jax
import jax.numpy as jnp
import numpy as np
from jax import lax
from jax.experimental import pallas as pl
from jax.experimental.pallas import tpu as pltpu
from jax.sharding import PartitionSpec as P

MESH = pl.DeviceIdType.MESH
EPS = 1e-06
ROPE_BASE = 1000000.0
GROUPS = 32
TENSOR = 4
ROWS = 32
ITEMS = 4
HEADS = 8
DIM = 128
WIDTH = 5120
QCOLS = HEADS * DIM
SLOTS = 1024
FLAT = 2 * ROWS
DEPTH = 2
SENDS = 2
SEND_COLS = QCOLS // SENDS
OUT_COLS = WIDTH // TENSOR
HALF_HEADS = HEADS // SENDS
HALF_ROWS = HALF_HEADS * 16
PIECES = 2
PIECE = WIDTH // PIECES
STEP_ROWS = HALF_HEADS * 8
SCALE = 1.0 / (DIM**0.5)
F32 = jnp.float32
BF16 = jnp.bfloat16


def dot_nt(a, b):
    return lax.dot_general(a, b, (((1,), (1,)), ((), ())), preferred_element_type=F32)


def dot_tn(a, b):
    return lax.dot_general(a, b, (((0,), (0,)), ((), ())), preferred_element_type=F32)


def kernel(
    len_hbm, slot_hbm, line_hbm, samp_hbm, gain_hbm, qg_hbm, kg_hbm, freq_hbm,
    x_hbm, wq_hbm, km_hbm, vm_hbm, wo_hbm, kc_hbm, vc_hbm,
    own_ref, rem_ref,
    len_ref, slot_ref, samp_ref, samp_v, gain, qg, kg, freq, small_sem, x_v, wq_v, km_v, vm_v, wo_v, kc_v, vc_v, vt_v, xs_v, nm_v, q_s,
    send_q, recv_q0, recv_q1, res_v, stat_v, last_v, send_r, recv_r, send_l, recv_l0, recv_l1,
    send_t, recv_t0, recv_t1, att_v, late_v, ofr_v, acc_v,
    sib_a, sib_b, part_a, part_b, part_c,
    x_sem, wq_sem, mat_sem, wo_sem, cache_sem,
    qs_sem, qr_sem, rs_sem, rr_sem, ls_sem, lr_sem, ss_sem, sr_sem, ts_sem, tr_sem,
):
    recv_q, recv_l, recv_t = (recv_q0, recv_q1), (recv_l0, recv_l1), (recv_t0, recv_t1)
    me = lax.axis_index("group")
    rank = lax.axis_index("tensor")
    core = lax.rem(rank, 2)
    chip = rank // 2
    sibling = chip * 2 + (1 - core)
    remote = (1 - chip) * 2 + core
    far = (1 - chip) * 2 + (1 - core)

    x_copy = pltpu.make_async_copy(x_hbm, x_v, x_sem)
    x_copy.start()
    wq_copies = [
        pltpu.make_async_copy(
            wq_hbm.at[pl.ds(n * PIECE, PIECE), pl.ds(s * SEND_COLS, SEND_COLS)],
            wq_v.at[s, pl.ds(n * PIECE, PIECE)],
            wq_sem.at[s, n],
        )
        for s in range(SENDS)
        for n in range(PIECES)
    ]
    for copy in wq_copies[:DEPTH]:
        copy.start()
    mat_copies = [
        pltpu.make_async_copy(km_hbm, km_v, mat_sem.at[0]),
        pltpu.make_async_copy(vm_hbm, vm_v, mat_sem.at[1]),
    ]

    small_copies = [
        pltpu.make_async_copy(source, target, small_sem.at[n])
        for n, (source, target) in enumerate(
            [
                (line_hbm, samp_ref),
                (slot_hbm, slot_ref),
                (len_hbm, len_ref),
                (freq_hbm, freq),
                (gain_hbm, gain),
                (qg_hbm, qg),
                (kg_hbm, kg),
                (samp_hbm, samp_v),
            ]
        )
    ]
    for copy in small_copies:
        copy.start()
    barrier = pltpu.get_barrier_semaphore()

    def greet(k, carry):
        pl.semaphore_signal(
            barrier, inc=1, device_id={"group": lax.rem(me + k, GROUPS)}, device_id_type=MESH
        )
        return carry

    lax.fori_loop(1, GROUPS, greet, 0)
    for other in (sibling, remote):
        pl.semaphore_signal(barrier, inc=1, device_id={"tensor": other}, device_id_type=MESH)

    for copy in small_copies[:3]:
        copy.wait()
    lane = lax.broadcasted_iota(jnp.int32, (1, FLAT), 1)
    sub = lax.broadcasted_iota(jnp.int32, (ROWS, FLAT), 0)
    key_lane = jnp.zeros((1, FLAT), jnp.int32)
    key_sub = jnp.zeros((ROWS, FLAT), jnp.int32)
    len_lane = jnp.zeros((1, FLAT), F32)
    row_of_lane = lax.rem(lane, ROWS)
    owners = []
    for r in range(ROWS):
        prompt = samp_ref[me * ROWS + r]
        owner = lax.shift_right_logical(slot_ref[prompt], 1)
        owners.append(owner)
        order_key = owner * ROWS + r
        key_lane = jnp.where(row_of_lane == r, order_key, key_lane)
        key_sub = jnp.where(sub == r, order_key, key_sub)
        len_lane = jnp.where(row_of_lane == r, len_ref[prompt].astype(F32), len_lane)
    place = jnp.sum((key_sub < key_lane).astype(jnp.int32), axis=0, keepdims=True)
    q_id = lax.broadcasted_iota(jnp.int32, (FLAT, FLAT), 0)
    c_id = lax.broadcasted_iota(jnp.int32, (FLAT, FLAT), 1)
    step_q = lax.rem(q_id // 8, 2)
    chosen = (step_q == c_id // ROWS) & ((q_id // 16) * 8 + lax.rem(q_id, 8) == place)
    sorter = jnp.where(chosen, 1.0, 0.0).astype(BF16)
    step_sorter = jnp.where(q_id[:ROWS, :ROWS] == place[:, :ROWS], 1.0, 0.0).astype(BF16)
    position = jnp.sum(jnp.where(chosen, len_lane, 0.0), axis=1, keepdims=True)
    position = position + step_q[:, :1].astype(F32)
    for copy in small_copies[3:]:
        copy.wait()
    angle = position * freq[...]
    cosine = jnp.cos(angle)
    half = lax.broadcasted_iota(jnp.int32, (FLAT, DIM), 1) < DIM // 2
    sine = jnp.sin(angle)
    sine = jnp.where(half, -sine, sine)

    def head(values, gains):
        mean = jnp.mean(values * values, axis=-1, keepdims=True)
        scaled = values * lax.rsqrt(mean + EPS) * gains
        return (scaled * cosine + pltpu.roll(scaled, DIM // 2, 1) * sine).astype(BF16)

    x_copy.wait()
    total = jnp.zeros((FLAT, 1), F32)
    for c in range(5):
        cols = slice(c * 1024, (c + 1) * 1024)
        part = jnp.dot(sorter, x_v[:, cols], preferred_element_type=F32)
        xs_v[:, cols] = part
        total = total + jnp.sum(part * part, axis=1, keepdims=True)
    item_owner = []
    floor = jnp.int32(-1)
    for _ in range(ITEMS):
        best = jnp.int32(GROUPS)
        for owner in owners:
            best = jnp.where((owner > floor) & (owner < best), owner, best)
        item_owner.append(best)
        floor = best

    scale = lax.rsqrt(total * (1.0 / WIDTH) + EPS)
    for c in range(5):
        cols = slice(c * 1024, (c + 1) * 1024)
        nm_v[:, cols] = (xs_v[:, cols] * scale * gain[:, cols]).astype(BF16)

    def shuffled(n):
        return lax.rem(n * 7, GROUPS - 1) + 1

    def item_for(dest):
        found = jnp.int32(0)
        for i in range(ITEMS - 1):
            found = found + (dest > item_owner[i]).astype(jnp.int32)
        return found

    for s in range(SENDS):
        raw = None
        for n in range(PIECES):
            at = s * PIECES + n
            wq_copies[at].wait()
            if at + DEPTH < len(wq_copies):
                wq_copies[at + DEPTH].start()
            elif at + DEPTH == len(wq_copies):
                for copy in mat_copies:
                    copy.start()
            rows = slice(n * PIECE, (n + 1) * PIECE)
            part = jnp.dot(nm_v[:, rows], wq_v[s, rows], preferred_element_type=F32)
            raw = part if raw is None else raw + part
        for h in range(HALF_HEADS):
            turned = head(raw[:, h * DIM : (h + 1) * DIM], qg[...])
            at = (s * HALF_HEADS + h) * DIM
            q_s[:, :, at : at + DIM] = turned.reshape(ITEMS, 16, DIM)
        if s == 0:
            pl.semaphore_wait(barrier, GROUPS - 1 + 2)
        cols = slice(s * SEND_COLS, (s + 1) * SEND_COLS)
        recv_q[s][0] = q_s[item_for(me), :, cols]

        def send(n, carry):
            k = shuffled(n)
            dest = lax.rem(me + k, GROUPS)
            send_q[s, k] = q_s[item_for(dest), :, cols]
            pltpu.make_async_remote_copy(
                src_ref=send_q.at[s, k],
                dst_ref=recv_q[s].at[k],
                send_sem=qs_sem.at[s],
                recv_sem=qr_sem.at[s],
                device_id={"group": dest},
                device_id_type=MESH,
            ).start()
            return carry

        lax.fori_loop(0, GROUPS - 1, send, 0)

    cache_copies = [
        pltpu.make_async_copy(kc_hbm, kc_v, cache_sem.at[0]),
        pltpu.make_async_copy(vc_hbm, vc_v, cache_sem.at[1]),
    ]
    for copy in cache_copies:
        copy.start()
    wo_copies = []
    for b, block in enumerate((far, remote, sibling, rank)):
        copy = pltpu.make_async_copy(
            wo_hbm.at[:, pl.ds(pl.multiple_of(block * OUT_COLS, OUT_COLS), OUT_COLS)],
            wo_v.at[b],
            wo_sem.at[b],
        )
        copy.start()
        wo_copies.append(copy)

    group_id = (
        lax.broadcasted_iota(jnp.int32, (8, 128), 0) * 4
        + lax.broadcasted_iota(jnp.int32, (8, 128), 1) // ROWS
    )
    limits, readers = [], []
    for p in range(2):
        prompt = jnp.int32(0)
        for i in range(64):
            prompt = jnp.where(slot_ref[i] == me * 2 + p, jnp.int32(i), prompt)
        limits.append(len_ref[prompt])
        hit = samp_v[...] == prompt
        readers.append(jnp.min(jnp.where(hit, group_id, GROUPS - 1)))
        readers.append(jnp.max(jnp.where(hit, group_id, 0)))


    for copy in mat_copies:
        copy.wait()
    fresh_key = head(jnp.dot(nm_v[...], km_v[...], preferred_element_type=F32), kg[...])
    fresh_value = jnp.dot(nm_v[...], vm_v[...], preferred_element_type=F32).astype(BF16)
    q_all = jnp.concatenate(
        [
            q_s[i, :, h * DIM : (h + 1) * DIM]
            for s in range(SENDS)
            for i in range(ITEMS)
            for h in range(s * HALF_HEADS, (s + 1) * HALF_HEADS)
        ],
        axis=0,
    )
    cells = (FLAT, ITEMS * DIM)
    row_id = lax.broadcasted_iota(jnp.int32, cells, 0)
    col_id = lax.broadcasted_iota(jnp.int32, cells, 1)
    seen = (
        (row_id // 16 == lax.rem(col_id // HALF_ROWS, ITEMS))
        & (lax.rem(row_id, 8) == lax.rem(col_id, 8))
        & (lax.rem(row_id // 8, 2) <= lax.rem(col_id // 8, 2))
    )
    fresh_score = jnp.where(seen, dot_nt(fresh_key, q_all) * SCALE, -1e30)
    fresh_peak = jnp.max(fresh_score, axis=0, keepdims=True)
    fresh_weight = jnp.where(seen, jnp.exp(fresh_score - fresh_peak), 0.0).astype(BF16)
    fresh_total = jnp.sum(fresh_weight.astype(F32), axis=0, keepdims=True)
    ofr_v[...] = dot_tn(fresh_weight, fresh_value)

    for copy in cache_copies:
        copy.wait()
    for p in range(2):
        vt_v[p] = vc_v[p].T

    key_id = lax.broadcasted_iota(jnp.int32, (SLOTS, DIM), 0)
    first_half = lax.broadcasted_iota(jnp.int32, (1, DIM), 1) < HALF_ROWS

    def result_for(dest):
        found = jnp.int32(0)
        for i in range(1, ITEMS):
            found = jnp.where(dest == readers[i], jnp.int32(i), found)
        return found

    for s in range(SENDS):
        pltpu.make_async_copy(
            send_q.at[s, pl.ds(1, GROUPS - 1)], recv_q[s].at[pl.ds(1, GROUPS - 1)], qr_sem.at[s]
        ).wait()
        for p in range(2):
            blocks = []
            for i in range(2):
                got = recv_q[s][lax.rem(me - readers[2 * p + i] + GROUPS, GROUPS)]
                blocks += [got[:, h * DIM : (h + 1) * DIM] for h in range(HALF_HEADS)]
            queries = jnp.concatenate(blocks, axis=0)
            valid = key_id < limits[p]
            score = jnp.where(valid, dot_nt(kc_v[p], queries) * SCALE, -1e30)
            peak = jnp.max(score, axis=0, keepdims=True)
            weight = jnp.where(valid, jnp.exp(score - peak), 0.0).astype(BF16)
            amount = jnp.sum(weight.astype(F32), axis=0, keepdims=True)
            summed = jnp.dot(vt_v[p], weight, preferred_element_type=F32).T
            for i in range(2):
                own = summed[i * HALF_ROWS : (i + 1) * HALF_ROWS]
                if s == 0:
                    res_v[2 * p + i] = own.astype(BF16)
                    continue
                for t in range(2):
                    rows = [own[h * 16 + t * 8 : h * 16 + t * 8 + 8] for h in range(HALF_HEADS)]
                    last_v[t, 2 * p + i] = jnp.concatenate(rows, axis=0).astype(BF16)
            peak_turned = pltpu.roll(peak, HALF_ROWS, 1)
            amount_turned = pltpu.roll(amount, HALF_ROWS, 1)
            stat_v[s, 2 * p] = jnp.where(first_half, peak, amount_turned)
            stat_v[s, 2 * p + 1] = jnp.where(first_half, peak_turned, amount)

        if s == 0:
            trips = [(res_v, send_r, recv_r, rs_sem, rr_sem)]
        else:
            trips = [
                (last_v.at[t], send_l.at[t], recv_l[t], ls_sem.at[t], lr_sem.at[t])
                for t in range(2)
            ]
        trips = [(stat_v.at[s], send_t.at[s], recv_t[s], ss_sem.at[s], sr_sem.at[s])] + trips
        for source, sent, got_back, send_sem, recv_sem in trips:
            got_back[0] = source[result_for(me)]

            def give_back(n, carry):
                k = shuffled(n)
                dest = lax.rem(me + k, GROUPS)
                sent[k] = source[result_for(dest)]
                pltpu.make_async_remote_copy(
                    src_ref=sent.at[k],
                    dst_ref=got_back.at[k],
                    send_sem=send_sem,
                    recv_sem=recv_sem,
                    device_id={"group": dest},
                    device_id_type=MESH,
                ).start()
                return carry

            lax.fori_loop(0, GROUPS - 1, give_back, 0)

    def wait_all(sent, got_back, sem):
        others = pl.ds(1, GROUPS - 1)
        pltpu.make_async_copy(sent.at[others], got_back.at[others], sem).wait()

    places = [lax.rem(me - owner + GROUPS, GROUPS) for owner in item_owner]
    factor_id = lax.broadcasted_iota(jnp.int32, (8, ITEMS * HALF_ROWS), 0)

    def factors_of(s):
        wait_all(send_t.at[s], recv_t[s], sr_sem.at[s])
        stats = [recv_t[s][at] for at in places]
        peak = jnp.concatenate([stat[:, :HALF_ROWS] for stat in stats], axis=1)
        amount = jnp.concatenate([stat[:, HALF_ROWS:] for stat in stats], axis=1)
        cols = slice(s * ITEMS * HALF_ROWS, (s + 1) * ITEMS * HALF_ROWS)
        own_peak = fresh_peak[:, cols]
        joint = jnp.maximum(peak, own_peak)
        early = jnp.exp(peak - joint)
        late = jnp.exp(own_peak - joint)
        lower = amount * early + fresh_total[:, cols] * late
        return jnp.where(factor_id == 0, early / lower, late / lower).T

    factors = factors_of(0)
    wait_all(send_r, recv_r, rr_sem)
    for i in range(ITEMS):
        rows = slice(i * HALF_ROWS, (i + 1) * HALF_ROWS)
        done = recv_r[places[i]].astype(F32) * factors[rows, 0:1] + ofr_v[rows] * factors[rows, 1:2]
        done = done.astype(BF16)
        for h in range(HALF_HEADS):
            att_v[i * 16 : (i + 1) * 16, h * DIM : (h + 1) * DIM] = done[h * 16 : (h + 1) * 16]
    attended = dot_tn(sorter, att_v[...]).astype(BF16)
    for block in range(TENSOR):
        wo_copies[block].wait()
        acc_v[block] = jnp.dot(
            attended, wo_v[block, : HALF_HEADS * DIM], preferred_element_type=F32
        )
    factors = factors_of(1)

    def merge_step(t):
        wait_all(send_l.at[t], recv_l[t], lr_sem.at[t])
        for i in range(ITEMS):
            got = recv_l[t][places[i]].astype(F32)
            for h in range(HALF_HEADS):
                at = i * HALF_ROWS + h * 16 + t * 8
                done = got[h * 8 : (h + 1) * 8] * factors[at : at + 8, 0:1]
                fresh = ofr_v[ITEMS * HALF_ROWS + at : ITEMS * HALF_ROWS + at + 8]
                late_v[t, i * 8 : (i + 1) * 8, h * DIM : (h + 1) * DIM] = (
                    done + fresh * factors[at : at + 8, 1:2]
                )
        return dot_tn(step_sorter, late_v[t].astype(BF16)).astype(BF16)

    def pass_on(n, source, target, device):
        return pltpu.make_async_remote_copy(
            src_ref=source,
            dst_ref=target,
            send_sem=ts_sem.at[n],
            recv_sem=tr_sem.at[n],
            device_id={"tensor": device},
            device_id_type=MESH,
        )

    first, second, third = [], [], []
    for t in range(2):
        attended = merge_step(t)

        def project(block):
            last = jnp.dot(
                attended, wo_v[block, HALF_HEADS * DIM :], preferred_element_type=F32
            )
            return acc_v[block, t * ROWS : (t + 1) * ROWS] + last

        part_a[t] = project(0).astype(BF16)
        first.append(pass_on(t, part_a.at[t], sib_a.at[t], sibling))
        first[t].start()
        mine = project(1)
        part_c[t] = project(2).astype(BF16)
        third.append(pass_on(4 + t, part_c.at[t], sib_b.at[t], sibling))
        third[t].start()
        first[t].wait_recv()
        part_b[t] = (mine + sib_a[t].astype(F32)).astype(BF16)
        second.append(pass_on(2 + t, part_b.at[t], rem_ref.at[t], remote))
        second[t].start()
        mine = project(3)
        third[t].wait_recv()
        own_ref[t] = mine + sib_b[t].astype(F32)
    for t in range(2):
        second[t].wait_recv()

    for copy in first + second + third:
        copy.wait_send()
    for s in range(SENDS):
        pltpu.make_async_copy(
            send_q.at[s, pl.ds(1, GROUPS - 1)], recv_q[s].at[pl.ds(1, GROUPS - 1)], qs_sem.at[s]
        ).wait()
    wait_all(send_r, recv_r, rs_sem)
    for s in range(2):
        wait_all(send_t.at[s], recv_t[s], ss_sem.at[s])
        wait_all(send_l.at[s], recv_l[s], ls_sem.at[s])


def shards(
    inputs,
    attn_gain,
    w_query,
    key_matrix,
    value_matrix,
    q_gain,
    k_gain,
    w_out,
    prompt_key_cache,
    prompt_value_cache,
    prompt_lengths,
    prompt_slot,
    sample_prompt,
):
    half = np.arange(DIM // 2, dtype=np.float64)
    frequency = ROPE_BASE ** (-(half * 2.0 / DIM))
    frequency = jnp.asarray(np.concatenate([frequency, frequency])[None, :], F32)
    vmem = pl.BlockSpec(memory_space=pltpu.VMEM)
    anywhere = pl.BlockSpec(memory_space=pl.ANY)
    dma = pltpu.SemaphoreType.DMA
    own, other = pl.pallas_call(
        kernel,
        out_shape=(
            pltpu.VMEM((2, ROWS, OUT_COLS), F32),
            pltpu.VMEM((2, ROWS, OUT_COLS), BF16),
        ),
        in_specs=[anywhere] * 15,
        out_specs=(vmem, vmem),
        scratch_shapes=[
            pltpu.SMEM((64,), jnp.int32),
            pltpu.SMEM((64,), jnp.int32),
            pltpu.SMEM((1024,), jnp.int32),
            pltpu.VMEM((8, 128), jnp.int32),
            pltpu.VMEM((1, WIDTH), F32),
            pltpu.VMEM((1, DIM), F32),
            pltpu.VMEM((1, DIM), F32),
            pltpu.VMEM((1, DIM), F32),
            dma((8,)),
            pltpu.VMEM((FLAT, WIDTH), BF16),
            pltpu.VMEM((SENDS, WIDTH, SEND_COLS), BF16),
            pltpu.VMEM((WIDTH, DIM), BF16),
            pltpu.VMEM((WIDTH, DIM), BF16),
            pltpu.VMEM((TENSOR, QCOLS, OUT_COLS), BF16),
            pltpu.VMEM((2, SLOTS, DIM), BF16),
            pltpu.VMEM((2, SLOTS, DIM), BF16),
            pltpu.VMEM((2, DIM, SLOTS), BF16),
            pltpu.VMEM((FLAT, WIDTH), F32),
            pltpu.VMEM((FLAT, WIDTH), BF16),
            pltpu.VMEM((ITEMS, 16, QCOLS), BF16),
            pltpu.VMEM((SENDS, GROUPS, 16, SEND_COLS), BF16),
            pltpu.VMEM((GROUPS, 16, SEND_COLS), BF16),
            pltpu.VMEM((GROUPS, 16, SEND_COLS), BF16),
            pltpu.VMEM((ITEMS, HALF_ROWS, DIM), BF16),
            pltpu.VMEM((SENDS, ITEMS, 1, DIM), F32),
            pltpu.VMEM((2, ITEMS, STEP_ROWS, DIM), BF16),
            pltpu.VMEM((GROUPS, HALF_ROWS, DIM), BF16),
            pltpu.VMEM((GROUPS, HALF_ROWS, DIM), BF16),
            pltpu.VMEM((2, GROUPS, STEP_ROWS, DIM), BF16),
            pltpu.VMEM((GROUPS, STEP_ROWS, DIM), BF16),
            pltpu.VMEM((GROUPS, STEP_ROWS, DIM), BF16),
            pltpu.VMEM((SENDS, GROUPS, 1, DIM), F32),
            pltpu.VMEM((GROUPS, 1, DIM), F32),
            pltpu.VMEM((GROUPS, 1, DIM), F32),
            pltpu.VMEM((FLAT, SEND_COLS), BF16),
            pltpu.VMEM((2, ROWS, SEND_COLS), F32),
            pltpu.VMEM((ITEMS * DIM, DIM), F32),
            pltpu.VMEM((TENSOR, FLAT, OUT_COLS), F32),
            pltpu.VMEM((2, ROWS, OUT_COLS), BF16),
            pltpu.VMEM((2, ROWS, OUT_COLS), BF16),
            pltpu.VMEM((2, ROWS, OUT_COLS), BF16),
            pltpu.VMEM((2, ROWS, OUT_COLS), BF16),
            pltpu.VMEM((2, ROWS, OUT_COLS), BF16),
            dma,
            dma((SENDS, PIECES)),
            dma((2,)),
            dma((TENSOR,)),
            dma((2,)),
            dma((SENDS,)),
            dma((SENDS,)),
            dma,
            dma,
            dma((2,)),
            dma((2,)),
            dma((SENDS,)),
            dma((SENDS,)),
            dma((6,)),
            dma((6,)),
        ],
        compiler_params=pltpu.CompilerParams(
            collective_id=0, has_side_effects=True, vmem_limit_bytes=56 * 1024 * 1024
        ),
    )(
        prompt_lengths,
        prompt_slot,
        sample_prompt,
        sample_prompt.reshape(8, 128),
        attn_gain.reshape(1, WIDTH),
        q_gain.reshape(1, DIM),
        k_gain.reshape(1, DIM),
        frequency,
        inputs.reshape(FLAT, WIDTH),
        w_query,
        key_matrix,
        value_matrix,
        w_out,
        prompt_key_cache,
        prompt_value_cache,
    )
    return (own + other.astype(F32)).astype(BF16)


def solution(mesh):
    in_specs = (
        P(None, "group", None),
        P(),
        P(None, "tensor"),
        P(None, "tensor"),
        P(None, "tensor"),
        P(),
        P(),
        P("tensor", None),
        P("group", None, "tensor"),
        P("group", None, "tensor"),
        P(),
        P(),
        P(),
    )
    out_specs = P(None, "group", "tensor")
    return jax.shard_map(shards, mesh=mesh, in_specs=in_specs, out_specs=out_specs, check_vma=False)
```
